256 devices in a mesh: group: 8 (over y, core), region: 32 (over x, z).
Axes of the slice: x: 4, y: 4, z: 8, core: 2. Of those that a mesh axis runs over, the one named last changes fastest.
Arguments:
- observed: float32 [524288], P(('group', 'region')), may hold values from -6 to 6
- noise_precision: float32 [524288], P(('group', 'region')), may hold values from 0.25 to 4
- mid_basis: float32 [524288, 512], P(('group', 'region')), may hold values from -0.038669902 to 0.038669902
- root_basis: float32 [524288, 512], P(('group', 'region')), may hold values from -0.013671875 to 0.013671875
- mid_prior: float32 [8, 512], P('group'), may hold values from 0.3 to 3
- root_prior: float32 [512], replicated, may hold values from 0.3 to 3
- leaf_count: int32 [8, 32], P('group', 'region'), may hold values from 1024 to 2048, as said below
Outputs:
- root_weight_means: float32 [512], replicated
- middle_weight_means: float32 [8, 512], P('group', 'region')
- leaf_fit: float32 [524288], P(('group', 'region'))
The draws below stay inside these ranges and needn't reach their ends.
Inputs may be any that keep to these rules, and one draw needn't show every extreme that they name: `leaf_count`: every entry lies between 1024 and 2048, and some region has all 2048 slots live.
All inputs are finite; a program needn't handle non-finite values.
Results may differ from the reference program's by a relative error of at most 0.0012.
Values sent between devices are 32-bit elements; how exact they have to be, the bound alone decides.
No kernel may reach another device: no remote copies, remote signals or barrier semaphores. Data moves between devices by JAX's collectives and lax.ppermute only.
A program may use at most 64 MiB of HBM per device.

```python
import math
import jax
import jax.numpy as jnp
from jax import lax

L = 2048
M = 512
R = 512
GROUPS = 8
REGIONS = 32
GROUP_OBS = 65536
OBS = 524288
N_GROUP = 8
N_REGION = 32


energy_level = 8.0


clip_level = 3.5


shared_part = 0.8


fresh_part = 0.6


mid_stretch_divisor = 1.5


root_stretch_divisor = 6.0


def draw_leaf_count(key, part):
    counts = jax.random.randint(key, (GROUPS * REGIONS,), L // 2, L + 1)
    chosen = jax.random.randint(jax.random.fold_in(key, 7), (), 0, GROUPS * REGIONS)
    counts = jnp.where(jnp.arange(GROUPS * REGIONS) == chosen, L, counts)
    return counts.reshape(GROUPS, REGIONS).astype(jnp.int32)


def knot_mixing(base_key, knot_count, divisor):
    points = jax.random.uniform(base_key, (knot_count, 2), jnp.float32)
    offsets = points[:, None, :] - points[None, :, :]
    distance = jnp.sqrt(jnp.sum(offsets * offsets, axis=-1))
    stretch = math.sqrt(knot_count) / divisor
    scaled = distance * stretch
    kernel = (1.0 + scaled) * jnp.exp(-scaled)
    return kernel / jnp.sqrt(jnp.sum(kernel * kernel, axis=0, keepdims=True))


def latent_block(row_key, width):
    return jax.random.normal(row_key, (GROUP_OBS, width), jnp.float32)


def shared_latent(key, group_index):
    return latent_block(jax.random.fold_in(jax.random.fold_in(key, 41), group_index), max(M, R))


def basis_rows(latent, mixing, spread):
    rows = jnp.dot(latent, mixing, precision=lax.Precision.HIGHEST, preferred_element_type=jnp.float32) * spread
    limit = clip_level * spread
    return jnp.clip(rows, -limit, limit)


def draw_mid_basis(key, part):
    base_key = jax.random.fold_in(key, 11)
    spread = math.sqrt(energy_level / GROUP_OBS)

    def one_group(group_index):
        mixing = knot_mixing(jax.random.fold_in(base_key, 2 * group_index + 1), M, mid_stretch_divisor)
        latent = shared_latent(key, group_index)[:, :M]
        return basis_rows(latent, mixing, spread)
    return lax.map(one_group, jnp.arange(GROUPS, dtype=jnp.int32)).reshape(OBS, M)


def draw_root_basis(key, part):
    base_key = jax.random.fold_in(key, 23)
    mixing = knot_mixing(jax.random.fold_in(key, 29), R, root_stretch_divisor)
    spread = math.sqrt(energy_level / OBS)

    def one_group(group_index):
        fresh = latent_block(jax.random.fold_in(base_key, group_index), R)
        latent = shared_part * shared_latent(key, group_index)[:, :R] + fresh_part * fresh
        return basis_rows(latent, mixing, spread)
    return lax.map(one_group, jnp.arange(GROUPS, dtype=jnp.int32)).reshape(OBS, R)


def levels(stream_key, dims, pieces, smallest, top_value):
    gain, own = 1.0, jax.random.fold_in(stream_key, 6)
    for position, blocks in pieces:
        draws = jnp.exp(jax.random.uniform(jax.random.fold_in(own, position), (blocks,), jnp.float32, smallest / len(pieces), top_value / len(pieces)))
        gain = gain * jnp.repeat(draws, dims[position] // blocks).reshape([-1 if axis == position else 1 for axis in range(len(dims))])
    return gain


def centred(key, dims, scale, most, shards=(), held_as=jnp.bfloat16):
    entries = scale * jax.random.normal(key, dims, jnp.float32)
    if shards:
        entries = entries * levels(key, dims, shards, -0.22, 0.18)
    return jnp.clip(entries, -most, most).astype(held_as)


def setup_inputs(seed: int = 0) -> dict:
    splits = jax.random.split(jax.random.key(seed), 8)
    return {
        "observed": centred(splits[0], (OBS,), 1.0, 6.0, ((0, 256),), jnp.float32),
        "noise_precision": jnp.clip(jnp.exp(math.log(4.0) - 2.7725887 * jax.random.uniform(splits[1], (OBS,), jnp.float32) ** levels(splits[1], (OBS,), ((0, 256),), -0.2, 0.2)), 0.25, 4.0),
        "mid_basis": draw_mid_basis(jax.random.fold_in(splits[7], 71), 0),
        "root_basis": draw_root_basis(jax.random.fold_in(splits[7], 71), 0),
        "mid_prior": jnp.clip(jnp.exp(math.log(3.0) - 2.3025851 * jax.random.uniform(splits[4], (GROUPS, M), jnp.float32) ** levels(splits[4], (GROUPS, M), ((0, 8),), -0.2, 0.2)), 0.3, 3.0),
        "root_prior": jnp.clip(jnp.exp(jax.random.uniform(splits[5], (R,), jnp.float32, math.log(0.3), math.log(3.0))), 0.3, 3.0),
        "leaf_count": draw_leaf_count(jax.random.fold_in(splits[7], 71), 0),
    }


highest_precision = lax.Precision.HIGHEST

def inner_gram(former, latter):
    return lax.dot_general(former.astype(jnp.float32), latter.astype(jnp.float32), (((0,), (0,)), ((), ())), precision=highest_precision, preferred_element_type=jnp.float32)

def cholesky_solve(factor, rhs):
    column = rhs.ndim == 1
    matrix = rhs[:, None] if column else rhs
    lower_solved = lax.linalg.triangular_solve(factor, matrix, left_side=True, lower=True)
    result = lax.linalg.triangular_solve(factor, lower_solved, left_side=True, lower=True, transpose_a=True)
    return result[:, 0] if column else result

def reference(observed, noise_precision, mid_basis, root_basis, mid_prior, root_prior, leaf_count):
    per_group = L * N_REGION
    live = (jnp.arange(L, dtype=jnp.int32)[None, None, :] < leaf_count[:, :, None]).astype(jnp.float32)
    weight = noise_precision.reshape(N_GROUP, per_group) * live.reshape(N_GROUP, per_group)
    values = observed.reshape(N_GROUP, per_group)
    mid_rows = mid_basis.reshape(N_GROUP, per_group, M)
    root_rows = root_basis.reshape(N_GROUP, per_group, R)

    def group_contributions(items):
        values_g, weight_g, mid_g, root_g, prior_g = items
        weighted_obs = values_g * weight_g
        weighted_mid = mid_g * weight_g[:, None]
        mid_gram = inner_gram(weighted_mid, mid_g) + jnp.diag(prior_g)
        cross = inner_gram(weighted_mid, root_g)
        mid_rhs = jnp.dot(weighted_obs.astype(jnp.float32), mid_g.astype(jnp.float32), precision=highest_precision, preferred_element_type=jnp.float32)
        root_gram = inner_gram(root_g * weight_g[:, None], root_g)
        root_rhs = jnp.dot(weighted_obs.astype(jnp.float32), root_g.astype(jnp.float32), precision=highest_precision, preferred_element_type=jnp.float32)
        factor = jnp.linalg.cholesky(mid_gram)
        solved_cross_terms = cholesky_solve(factor, cross)
        solved_right_hand = cholesky_solve(factor, mid_rhs)
        reduced_gram = root_gram - inner_gram(cross, solved_cross_terms)
        reduced_rhs = root_rhs - jnp.dot(solved_right_hand.astype(jnp.float32), cross.astype(jnp.float32), precision=highest_precision, preferred_element_type=jnp.float32)
        return (reduced_gram, reduced_rhs, solved_cross_terms, solved_right_hand)
    reduced_gram, reduced_rhs, solved_cross_terms, solved_right_hand = lax.map(group_contributions, (values, weight, mid_rows, root_rows, mid_prior))
    root_matrix = jnp.sum(reduced_gram, axis=0) + jnp.diag(root_prior)
    root_vector = jnp.sum(reduced_rhs, axis=0)
    root_factor = jnp.linalg.cholesky(root_matrix)
    root_weight_means = cholesky_solve(root_factor, root_vector)
    middle_weight_means = solved_right_hand - jnp.einsum('wok,k->wo', solved_cross_terms, root_weight_means, precision=highest_precision)
    fit_mid = jnp.einsum('gnm,gm->gn', mid_rows, middle_weight_means, precision=highest_precision).reshape(-1)
    fit_root = jnp.dot(root_basis.astype(jnp.float32), root_weight_means.astype(jnp.float32), precision=highest_precision, preferred_element_type=jnp.float32)
    return (root_weight_means, middle_weight_means, fit_mid + fit_root)
```

```python
import functools

import jax
import jax.numpy as jnp
from jax import lax
from jax.experimental import pallas as pl
from jax.experimental.pallas import tpu as pltpu
from jax.sharding import PartitionSpec as P

f32, bf16 = jnp.float32, jnp.bfloat16
BLOCK = 128
TILE = 8
VMEM_LIMIT = 40 * 1024 * 1024


def whole(count):
    return [pl.BlockSpec(memory_space=pltpu.VMEM)] * count


def lower_blocks(blocks):
    return [(i, j) for i in range(blocks) for j in range(i + 1)]


def product(a, b, dims):
    return lax.dot_general(
        a, b, (dims, ((), ())), precision=lax.Precision.HIGHEST, preferred_element_type=f32
    )


def mm(a, b):
    return product(a, b, ((1,), (0,)))


def mm_t(a, b):
    return product(a, b, ((1,), (1,)))


def t_mm(a, b):
    return product(a, b, ((0,), (0,)))


def halves(value):
    high = value.astype(bf16)
    return high, (value - high.astype(f32)).astype(bf16)


def bf_t_mm(a, b):
    return lax.dot_general(a, b, (((0,), (0,)), ((), ())), preferred_element_type=f32)


def weights_in_columns(count_ref, noise_ref, observed_ref):
    chunks = noise_ref.shape[0]
    slot = lax.broadcasted_iota(jnp.int32, (chunks, BLOCK), 0) * BLOCK + lax.broadcasted_iota(
        jnp.int32, (chunks, BLOCK), 1
    )
    weight = jnp.where(slot < count_ref[0, 0], noise_ref[...], 0.0)
    root = jnp.sqrt(weight)
    seen = root * observed_ref[...]
    stacked = jnp.concatenate([root, seen] * (BLOCK // (2 * chunks)), axis=0)
    turned = stacked.T
    return (
        [turned[:, c : c + 1] for c in range(chunks)],
        [turned[:, chunks + c : chunks + c + 1] for c in range(chunks)],
    )


def scaled_rows(rows_ref, start, columns, scaled_obs):
    rows, sums = [], 0.0
    for c, y in zip(columns, scaled_obs):
        part = rows_ref[start : start + BLOCK, :] * c
        sums = sums + jnp.sum((part * y).reshape(-1, TILE, part.shape[1]), axis=0)
        rows.append(part)
        start += BLOCK
    return jnp.concatenate(rows, axis=0), sums


def rows_of(vector, rows):
    line = jnp.sum(vector, axis=0, keepdims=True)
    row = lax.broadcasted_iota(jnp.int32, (rows, BLOCK), 0)
    out = jnp.zeros((rows, BLOCK), f32)
    for k in range(vector.shape[1] // BLOCK):
        out = jnp.where(row == k, line[:, k * BLOCK : (k + 1) * BLOCK], out)
    return out


def store_lower(matrix, out_ref, tiles_each):
    number = 0
    for i, j in lower_blocks(matrix.shape[0] // BLOCK):
        block = matrix[i * BLOCK : (i + 1) * BLOCK, j * BLOCK : (j + 1) * BLOCK]
        for t in range(BLOCK // TILE):
            at = TILE * (number % tiles_each)
            out_ref[number // tiles_each, at : at + TILE, :] = block[t * TILE : (t + 1) * TILE, :]
            number += 1


def load_tile(ref, block, t, tiles_each):
    number = block * (BLOCK // TILE) + t
    at = TILE * (number % tiles_each)
    return ref[number // tiles_each, at : at + TILE, :]


def load_block(ref, block, tiles_each):
    return jnp.concatenate(
        [load_tile(ref, block, t, tiles_each) for t in range(BLOCK // TILE)], axis=0
    )


def start_copies(source_ref, held_ref, sems, pieces):
    size = source_ref.shape[0] // pieces
    copies = []
    for p in range(pieces):
        copy = pltpu.make_async_copy(
            source_ref.at[pl.ds(p * size, size), :], held_ref.at[pl.ds(p * size, size), :], sems.at[p]
        )
        copy.start()
        copies.append(copy)
    return copies


def mid_gram_kernel(pieces, count_ref, noise_ref, observed_ref, mid_ref, out_ref, held, both, cross, sems):
    copies = start_copies(mid_ref, held, sems, pieces)
    columns, scaled_obs = weights_in_columns(count_ref, noise_ref, observed_ref)
    each = len(columns) // pieces
    rhs = 0.0
    for p in range(pieces):
        copies[p].wait()
        rows, sums = scaled_rows(
            held, p * each * BLOCK, columns[p * each : (p + 1) * each], scaled_obs[p * each : (p + 1) * each]
        )
        rhs = rhs + sums
        high, low = halves(rows)
        if p == 0:
            both[...] = bf_t_mm(high, high)
            cross[...] = bf_t_mm(high, low)
        else:
            both[...] += bf_t_mm(high, high)
            cross[...] += bf_t_mm(high, low)
    tiles_each = (out_ref.shape[1] - TILE) // TILE
    store_lower(both[...] + (cross[...] + cross[...].T), out_ref, tiles_each)
    line = rows_of(rhs, TILE)
    for r in range(out_ref.shape[0]):
        out_ref[r, tiles_each * TILE :, :] = line


def root_gram_kernel(
    pieces, count_ref, noise_ref, observed_ref, mid_ref, root_ref, out_ref, gram_ref, held_mid, held_root, total, both, cross, sems_mid, sems_root
):
    copies_mid = start_copies(mid_ref, held_mid, sems_mid, pieces)
    copies_root = start_copies(root_ref, held_root, sems_root, pieces)
    columns, scaled_obs = weights_in_columns(count_ref, noise_ref, observed_ref)
    each = len(columns) // pieces
    rhs = 0.0
    for p in range(pieces):
        copies_mid[p].wait()
        copies_root[p].wait()
        own = slice(p * each, (p + 1) * each)
        mid_rows = jnp.concatenate(
            [
                held_mid[(p * each + c) * BLOCK : (p * each + c + 1) * BLOCK, :] * columns[p * each + c]
                for c in range(each)
            ],
            axis=0,
        )
        root_rows, sums = scaled_rows(held_root, p * each * BLOCK, columns[own], scaled_obs[own])
        rhs = rhs + sums
        mid_high, mid_low = halves(mid_rows)
        root_high, root_low = halves(root_rows)
        product_now = bf_t_mm(mid_high, root_high) + (
            bf_t_mm(mid_high, root_low) + bf_t_mm(mid_low, root_high)
        )
        both_now, cross_now = bf_t_mm(root_high, root_high), bf_t_mm(root_high, root_low)
        if p == 0:
            total[...], both[...], cross[...] = product_now, both_now, cross_now
        else:
            total[...] += product_now
            both[...] += both_now
            cross[...] += cross_now
    regions = out_ref.shape[0]
    slab = total.shape[0] // regions
    blocks = total.shape[1] // BLOCK
    for j in range(blocks):
        out_ref[:, j * slab : (j + 1) * slab, :] = total[:, j * BLOCK : (j + 1) * BLOCK].reshape(
            regions, slab, BLOCK
        )
    line = rows_of(rhs, TILE)
    for r in range(regions):
        out_ref[r, blocks * slab :, :] = line
    store_lower(both[...] + (cross[...] + cross[...].T), gram_ref, gram_ref.shape[1] // TILE)


def on_lanes(tile, lane):
    return jnp.broadcast_to(tile[:, lane : lane + 1], (TILE, BLOCK))


def negated_inverse(tiles):
    lane = lax.broadcasted_iota(jnp.int32, (TILE, BLOCK), 1)
    sub = lax.broadcasted_iota(jnp.int32, (TILE, BLOCK), 0)
    tiles = list(tiles)
    count = len(tiles)
    for t in range(count):
        base = TILE * t
        inside = (lane >= base) & (lane < base + TILE)
        rows = [jnp.broadcast_to(tiles[t][s : s + 1, :], (TILE, BLOCK)) for s in range(TILE)]
        d = [[None] * TILE for _ in range(TILE)]
        for s in range(TILE):
            for j in range(s, TILE):
                d[s][j] = d[j][s] = on_lanes(rows[s], base + j)
        rows = [
            jnp.where(inside, jnp.where(lane == base + s, 1.0, 0.0), rows[s]) for s in range(TILE)
        ]
        for s in range(TILE):
            inverse = 1.0 / d[s][s]
            for i in range(TILE):
                if i == s:
                    continue
                factor = d[i][s] * inverse
                for j in range(s + 1, TILE):
                    d[i][j] = d[i][j] - factor * d[s][j]
                rows[i] = rows[i] - factor * rows[s]
            rows[s] = rows[s] * inverse
            for j in range(s + 1, TILE):
                d[s][j] = d[s][j] * inverse
        rows = [jnp.where(inside, -row, row) for row in rows]
        new = rows[0]
        for s in range(1, TILE):
            new = jnp.where(sub == s, rows[s], new)
        for k in range(1, count):
            i = (t + k) % count
            parts = [on_lanes(tiles[i], base + j) * rows[j] for j in range(TILE)]
            while len(parts) > 1:
                parts = [a + b for a, b in zip(parts[::2], parts[1::2])]
            tiles[i] = jnp.where(inside, 0.0, tiles[i]) - parts[0]
        tiles[t] = new
    return tiles


def block_inverse(block):
    tiles = negated_inverse([block[t * TILE : (t + 1) * TILE, :] for t in range(BLOCK // TILE)])
    return jnp.concatenate([-tile for tile in tiles], axis=0)


def with_diagonal(block, prior):
    row = lax.broadcasted_iota(jnp.int32, (BLOCK, BLOCK), 0)
    lane = lax.broadcasted_iota(jnp.int32, (BLOCK, BLOCK), 1)
    return block + jnp.where(row == lane, prior, 0.0)


def all_rows(ref, row):
    return jnp.broadcast_to(ref[row : row + 1, :], (TILE, BLOCK))


def packed_rows(lines):
    row = lax.broadcasted_iota(jnp.int32, (TILE, BLOCK), 0)
    out = jnp.zeros((TILE, BLOCK), f32)
    for k, line in enumerate(lines):
        out = jnp.where(row == k, line, out)
    return out


def mid_kernel(
    gram_ref, cross_ref, rhs_ref, root_rhs_ref, prior_ref, out_ref, solved_ref, factor_ref, line_ref, left, schur
):
    blocks = prior_ref.shape[1] // BLOCK
    width = BLOCK * blocks
    each = BLOCK * blocks // cross_ref.shape[0]
    share = BLOCK // each
    order = {pair: n for n, pair in enumerate(lower_blocks(blocks))}
    gram = {pair: load_block(gram_ref, n, (gram_ref.shape[1] - TILE) // TILE) for pair, n in order.items()}
    for j in range(blocks):
        for k in range(blocks):
            left[k * BLOCK : (k + 1) * BLOCK, j * BLOCK : (j + 1) * BLOCK] = cross_ref[
                k * share : (k + 1) * share, j * each : (j + 1) * each, :
            ].reshape(BLOCK, BLOCK)
    lines = [all_rows(rhs_ref, k) for k in range(blocks)]
    vector = jnp.zeros((TILE, width), f32)
    number = 0
    for k in range(blocks):
        prior = prior_ref[:, k * BLOCK : (k + 1) * BLOCK]
        inverse = block_inverse(with_diagonal(gram[k, k], prior))
        now = left[k * BLOCK : (k + 1) * BLOCK, :]
        solved = mm(inverse, now)
        solved_ref[k * BLOCK : (k + 1) * BLOCK, :] = solved
        line = mm(lines[k], inverse)
        line_ref[k * TILE : (k + 1) * TILE, :] = line
        factors = {}
        for i in range(k + 1, blocks):
            factors[i] = mm(gram[i, k], inverse)
            factor_ref[number * BLOCK : (number + 1) * BLOCK, :] = factors[i]
            number += 1
            for j in range(k + 1, i + 1):
                gram[i, j] = gram[i, j] - mm_t(factors[i], gram[j, k])
            lines[i] = lines[i] - mm_t(line, gram[i, k])
            left[i * BLOCK : (i + 1) * BLOCK, :] -= mm(gram[i, k], solved)
        vector = vector - mm(line, now)
        for i in range(blocks):
            part = t_mm(now[:, i * BLOCK : (i + 1) * BLOCK], solved[:, : (i + 1) * BLOCK])
            own = (slice(i * BLOCK, (i + 1) * BLOCK), slice(0, (i + 1) * BLOCK))
            if k == 0:
                schur[own] = -part
            else:
                schur[own] -= part
    groups = out_ref.shape[0]
    tiles_each = (out_ref.shape[1] - TILE) // TILE
    store_lower(schur, out_ref, tiles_each)
    packed = root_rhs_ref[...] + packed_rows(
        [vector[:, k * BLOCK : (k + 1) * BLOCK] for k in range(blocks)]
    )
    for g in range(groups):
        out_ref[g, tiles_each * TILE :, :] = packed


def back_kernel(solved_ref, factor_ref, line_ref, full_ref, vector_ref):
    blocks = solved_ref.shape[0] // BLOCK
    pairs = [(k, i) for k in range(blocks) for i in range(k + 1, blocks)]
    order = {pair: n for n, pair in enumerate(pairs)}
    for k in reversed(range(blocks)):
        full = solved_ref[k * BLOCK : (k + 1) * BLOCK, :]
        line = line_ref[k * TILE : (k + 1) * TILE, :]
        for i in range(k + 1, blocks):
            n = order[k, i]
            factor = factor_ref[n * BLOCK : (n + 1) * BLOCK, :]
            full = full - t_mm(factor, full_ref[i * BLOCK : (i + 1) * BLOCK, :])
            line = line - mm(vector_ref[:, i * BLOCK : (i + 1) * BLOCK], factor)
        full_ref[k * BLOCK : (k + 1) * BLOCK, :] = full
        vector_ref[:, k * BLOCK : (k + 1) * BLOCK] = line


def root_kernel(
    pieces, gram_ref, rhs_ref, prior_ref, full_ref, vector_ref, mid_ref, root_ref, root_out, mid_out, fit_ref, held_mid, held_root, sems_mid, sems_root
):
    copies_mid = start_copies(mid_ref, held_mid, sems_mid, pieces)
    copies_root = start_copies(root_ref, held_root, sems_root, pieces)
    blocks = prior_ref.shape[1] // BLOCK
    tiles_each = gram_ref.shape[1] // TILE
    gram = {pair: load_block(gram_ref, n, tiles_each) for n, pair in enumerate(lower_blocks(blocks))}
    lines = [all_rows(rhs_ref, k) for k in range(blocks)]
    factors = {}
    for k in range(blocks):
        prior = prior_ref[:, k * BLOCK : (k + 1) * BLOCK]
        inverse = block_inverse(with_diagonal(gram[k, k], prior))
        solved = mm(lines[k], inverse)
        for i in range(k + 1, blocks):
            factors[i, k] = mm(gram[i, k], inverse)
            for j in range(k + 1, i + 1):
                gram[i, j] = gram[i, j] - mm_t(factors[i, k], gram[j, k])
            lines[i] = lines[i] - mm_t(solved, gram[i, k])
        lines[k] = solved
    for k in reversed(range(blocks)):
        for i in range(k + 1, blocks):
            lines[k] = lines[k] - mm(lines[i], factors[i, k])
    means = jnp.concatenate(lines, axis=1)
    root_out[...] = means[:1, :]
    middle = vector_ref[...] - mm_t(means, full_ref[...])
    mid_out[...] = middle[:1, :]
    ones = jnp.ones((TILE, BLOCK), f32)
    each = held_mid.shape[0] // pieces
    for p in range(pieces):
        copies_mid[p].wait()
        copies_root[p].wait()
        for c in range(each // BLOCK):
            at = p * each + c * BLOCK
            total = 0.0
            for k in range(blocks):
                own = slice(k * BLOCK, (k + 1) * BLOCK)
                total = total + held_mid[at : at + BLOCK, own] * middle[:1, own]
                total = total + held_root[at : at + BLOCK, own] * means[:1, own]
            fit_ref[at // BLOCK : at // BLOCK + 1, :] = mm_t(ones, total)[:1, :]


def exchange(value, axis):
    return lax.all_to_all(value, axis, 0, 0, tiled=True)


def for_everyone(value, axis):
    return jnp.broadcast_to(value[None], (lax.axis_size(axis), *value.shape))


def on_device(observed, noise_precision, mid_basis, root_basis, mid_prior, root_prior, leaf_count):
    slots, knots = mid_basis.shape
    root_knots = root_basis.shape[1]
    regions, groups = lax.axis_size("region"), lax.axis_size("group")
    chunks = slots // BLOCK
    noise = noise_precision.reshape(chunks, BLOCK)
    values = observed.reshape(chunks, BLOCK)
    blocks = knots // BLOCK
    packed = len(lower_blocks(blocks)) * BLOCK
    share = packed // regions
    group_share = packed // groups
    slab = knots // regions * (root_knots // BLOCK)
    params = pltpu.CompilerParams(vmem_limit_bytes=VMEM_LIMIT)
    pieces = 4
    smem = pl.BlockSpec(memory_space=pltpu.SMEM)
    far = pl.BlockSpec(memory_space=pl.ANY)
    square = pltpu.VMEM((knots, knots), f32)
    rows = pltpu.VMEM((slots, knots), f32)
    waits = pltpu.SemaphoreType.DMA((pieces,))

    def cost(flops, size):
        return pl.CostEstimate(flops=int(flops), bytes_accessed=int(size), transcendentals=0)

    gram_flops = 2 * slots * knots * knots
    mid_parts = pl.pallas_call(
        functools.partial(mid_gram_kernel, pieces),
        out_shape=jax.ShapeDtypeStruct((regions, share + TILE, BLOCK), f32),
        in_specs=[smem] + whole(2) + [far],
        out_specs=pl.BlockSpec(memory_space=pltpu.VMEM),
        scratch_shapes=[rows, square, square, waits],
        compiler_params=params,
        cost_estimate=cost(2 * gram_flops, 4 * slots * knots),
        name="mid_gram",
    )(leaf_count, noise, values, mid_basis)
    mid_shares = exchange(mid_parts, "region").sum(axis=0)

    cross_parts, root_parts = pl.pallas_call(
        functools.partial(root_gram_kernel, pieces),
        out_shape=(
            jax.ShapeDtypeStruct((regions, slab + TILE, BLOCK), f32),
            jax.ShapeDtypeStruct((groups, group_share, BLOCK), f32),
        ),
        in_specs=[smem] + whole(2) + [far, far],
        out_specs=tuple(whole(2)),
        scratch_shapes=[rows, rows, square, square, square, waits, waits],
        compiler_params=params,
        cost_estimate=cost(5 * gram_flops, 8 * slots * knots),
        name="root_gram",
    )(leaf_count, noise, values, mid_basis, root_basis)
    cross_shares = exchange(cross_parts, "region").sum(axis=0)
    root_share = exchange(root_parts, "group").sum(axis=0)
    fine = group_share // regions
    root_pieces = jnp.pad(root_share.reshape(regions, fine, BLOCK), ((0, 0), (0, TILE - fine), (0, 0)))

    mid_all = exchange(
        jnp.concatenate([for_everyone(mid_shares[:share], "region"), root_pieces], axis=1), "region"
    )
    root_piece = mid_all[:, share:].sum(axis=0)
    cross_all = exchange(
        for_everyone(jnp.concatenate([cross_shares[:slab], root_piece]), "region"), "region"
    )
    root_part = cross_all[:, slab : slab + fine].reshape(group_share, BLOCK)

    pairs = blocks * (blocks - 1) // 2
    reduced, solved, factor, line = pl.pallas_call(
        mid_kernel,
        out_shape=(
            jax.ShapeDtypeStruct((groups, group_share + TILE, BLOCK), f32),
            jax.ShapeDtypeStruct((knots, root_knots), f32),
            jax.ShapeDtypeStruct((pairs * BLOCK, BLOCK), f32),
            jax.ShapeDtypeStruct((blocks * TILE, BLOCK), f32),
        ),
        in_specs=whole(5),
        out_specs=tuple(whole(4)),
        scratch_shapes=[square, square],
        compiler_params=params,
        cost_estimate=cost(2.5e10, 4e6),
        name="mid_elimination",
    )(mid_all, cross_all, mid_shares[share:], cross_shares[slab:], mid_prior)

    summed = exchange(reduced, "group").sum(axis=0)
    full, vector = pl.pallas_call(
        back_kernel,
        out_shape=(
            jax.ShapeDtypeStruct((knots, root_knots), f32),
            jax.ShapeDtypeStruct((TILE, knots), f32),
        ),
        in_specs=whole(3),
        out_specs=tuple(whole(2)),
        compiler_params=params,
        cost_estimate=cost(4e9, 3e6),
        name="mid_back_substitution",
    )(solved, factor, line)
    root_all = exchange(for_everyone(summed[:group_share] + root_part, "group"), "group")

    root_means, mid_means, fit = pl.pallas_call(
        functools.partial(root_kernel, pieces),
        out_shape=(
            jax.ShapeDtypeStruct((1, root_knots), f32),
            jax.ShapeDtypeStruct((1, knots), f32),
            jax.ShapeDtypeStruct((chunks, BLOCK), f32),
        ),
        in_specs=whole(5) + [far, far],
        out_specs=tuple(whole(3)),
        scratch_shapes=[rows, rows, waits, waits],
        compiler_params=params,
        cost_estimate=cost(2.5e10, 8 * slots * knots),
        name="root_solve_and_fit",
    )(root_all, summed[group_share:], root_prior.reshape(1, root_knots), full, vector, mid_basis, root_basis)

    mid_slab = knots // regions
    middle = lax.dynamic_slice_in_dim(mid_means, lax.axis_index("region") * mid_slab, mid_slab, 1)
    return root_means.reshape(root_knots), middle, fit.reshape(slots)


def solution(mesh):
    return jax.shard_map(
        on_device,
        mesh=mesh,
        in_specs=(
            P(("group", "region")),
            P(("group", "region")),
            P(("group", "region"), None),
            P(("group", "region"), None),
            P("group", None),
            P(),
            P("group", "region"),
        ),
        out_specs=(P(), P("group", "region"), P(("group", "region"))),
        check_vma=False,
    )
```

```python
import functools

import jax
import jax.numpy as jnp
from jax import lax
from jax.experimental import pallas as pl
from jax.experimental.pallas import tpu as pltpu
from jax.sharding import PartitionSpec as P

f32, bf16 = jnp.float32, jnp.bfloat16
BLOCK = 128
TILE = 8
VMEM_LIMIT = 56 * 1024 * 1024


def whole(count):
    return [pl.BlockSpec(memory_space=pltpu.VMEM)] * count


def lower_blocks(blocks):
    return [(i, j) for i in range(blocks) for j in range(i + 1)]


def product(a, b, dims):
    return lax.dot_general(
        a, b, (dims, ((), ())), precision=lax.Precision.HIGHEST, preferred_element_type=f32
    )


def mm(a, b):
    return product(a, b, ((1,), (0,)))


def mm_t(a, b):
    return product(a, b, ((1,), (1,)))


def t_mm(a, b):
    return product(a, b, ((0,), (0,)))


def halves(value):
    high = value.astype(bf16)
    return high, (value - high.astype(f32)).astype(bf16)


def bf_t_mm(a, b):
    return lax.dot_general(a, b, (((0,), (0,)), ((), ())), preferred_element_type=f32)


def weights_in_columns(count_ref, noise_ref, observed_ref):
    chunks = noise_ref.shape[0]
    slot = lax.broadcasted_iota(jnp.int32, (chunks, BLOCK), 0) * BLOCK + lax.broadcasted_iota(
        jnp.int32, (chunks, BLOCK), 1
    )
    weight = jnp.where(slot < count_ref[0, 0], noise_ref[...], 0.0)
    root = jnp.sqrt(weight)
    seen = root * observed_ref[...]
    stacked = jnp.concatenate([root, seen] * (BLOCK // (2 * chunks)), axis=0)
    turned = stacked.T
    return (
        [turned[:, c : c + 1] for c in range(chunks)],
        [turned[:, chunks + c : chunks + c + 1] for c in range(chunks)],
    )


def scaled_rows(rows_ref, start, columns, scaled_obs):
    rows, sums = [], 0.0
    for c, y in zip(columns, scaled_obs):
        part = rows_ref[start : start + BLOCK, :] * c
        sums = sums + jnp.sum((part * y).reshape(-1, TILE, part.shape[1]), axis=0)
        rows.append(part)
        start += BLOCK
    return jnp.concatenate(rows, axis=0), sums


def rows_of(vectors):
    row = lax.broadcasted_iota(jnp.int32, (TILE, BLOCK), 0)
    out, at = jnp.zeros((TILE, BLOCK), f32), 0
    for vector in vectors:
        line = jnp.sum(vector, axis=0, keepdims=True)
        for k in range(vector.shape[1] // BLOCK):
            out = jnp.where(row == at, line[:, k * BLOCK : (k + 1) * BLOCK], out)
            at += 1
    return out


def store_lower(matrix, out_ref, tiles_each, first=0):
    number = 0
    for i, j in lower_blocks(matrix.shape[0] // BLOCK):
        block = matrix[i * BLOCK : (i + 1) * BLOCK, j * BLOCK : (j + 1) * BLOCK]
        for t in range(BLOCK // TILE):
            at = first + TILE * (number % tiles_each)
            out_ref[number // tiles_each, at : at + TILE, :] = block[t * TILE : (t + 1) * TILE, :]
            number += 1


def load_tile(ref, block, t, tiles_each):
    number = block * (BLOCK // TILE) + t
    at = TILE * (number % tiles_each)
    return ref[number // tiles_each, at : at + TILE, :]


def load_block(ref, block, tiles_each):
    return jnp.concatenate(
        [load_tile(ref, block, t, tiles_each) for t in range(BLOCK // TILE)], axis=0
    )


def start_copies(source_ref, held_ref, sems, pieces):
    size = source_ref.shape[0] // pieces
    copies = []
    for p in range(pieces):
        copy = pltpu.make_async_copy(
            source_ref.at[pl.ds(p * size, size), :], held_ref.at[pl.ds(p * size, size), :], sems.at[p]
        )
        copy.start()
        copies.append(copy)
    return copies


def gram_kernel(
    pieces, count_ref, noise_ref, observed_ref, mid_ref, root_ref, out_ref, root_out, held_mid, held_root, by_mid, by_low, by_root, sems_mid, sems_root
):
    copies_mid = start_copies(mid_ref, held_mid, sems_mid, pieces)
    copies_root = start_copies(root_ref, held_root, sems_root, pieces)
    columns, scaled_obs = weights_in_columns(count_ref, noise_ref, observed_ref)
    each = len(columns) // pieces
    knots, root_knots = mid_ref.shape[1], root_ref.shape[1]
    mid_rhs, root_rhs = 0.0, 0.0
    for p in range(pieces):
        own = slice(p * each, (p + 1) * each)
        copies_mid[p].wait()
        mid_rows, mid_sums = scaled_rows(held_mid, p * each * BLOCK, columns[own], scaled_obs[own])
        copies_root[p].wait()
        root_rows, root_sums = scaled_rows(held_root, p * each * BLOCK, columns[own], scaled_obs[own])
        mid_rhs, root_rhs = mid_rhs + mid_sums, root_rhs + root_sums
        mid_high, mid_low = halves(mid_rows)
        root_high, root_low = halves(root_rows)
        root_both = jnp.concatenate([root_high, root_low], axis=1)
        products = (
            bf_t_mm(mid_high, jnp.concatenate([mid_high, mid_low, root_both], axis=1)),
            bf_t_mm(mid_low, root_high),
            bf_t_mm(root_high, root_both),
        )
        for ref, value in zip((by_mid, by_low, by_root), products):
            if p == 0:
                ref[...] = value
            else:
                ref[...] += value
    cross = by_mid[:, knots : 2 * knots]
    regions = out_ref.shape[0]
    slab = knots // regions
    cross_rows = slab * (root_knots // BLOCK)
    tiles_each = (out_ref.shape[1] - TILE - cross_rows) // TILE
    store_lower(by_mid[:, :knots] + (cross + cross.T), out_ref, tiles_each, TILE)
    line = rows_of([mid_rhs, root_rhs])
    for r in range(regions):
        out_ref[r, :TILE, :] = line
    first = TILE * (1 + tiles_each)
    for j in range(root_knots // BLOCK):
        own = slice(j * BLOCK, (j + 1) * BLOCK)
        high = by_mid[:, 2 * knots + j * BLOCK : 2 * knots + (j + 1) * BLOCK]
        low = by_mid[:, 2 * knots + root_knots + j * BLOCK : 2 * knots + root_knots + (j + 1) * BLOCK]
        block = high + (low + by_low[:, own])
        at = first + j * slab
        out_ref[:, at : at + slab, :] = block.reshape(regions, slab, BLOCK)
    cross = by_root[:, root_knots:]
    store_lower(by_root[:, :root_knots] + (cross + cross.T), root_out, root_out.shape[1] // TILE)


def on_lanes(tile, lane):
    return jnp.broadcast_to(tile[:, lane : lane + 1], (TILE, BLOCK))


def negated_inverse(tiles):
    lane = lax.broadcasted_iota(jnp.int32, (TILE, BLOCK), 1)
    sub = lax.broadcasted_iota(jnp.int32, (TILE, BLOCK), 0)
    tiles = list(tiles)
    count = len(tiles)
    for t in range(count):
        base = TILE * t
        inside = (lane >= base) & (lane < base + TILE)
        rows = [jnp.broadcast_to(tiles[t][s : s + 1, :], (TILE, BLOCK)) for s in range(TILE)]
        d = [[None] * TILE for _ in range(TILE)]
        for s in range(TILE):
            for j in range(s, TILE):
                d[s][j] = d[j][s] = on_lanes(rows[s], base + j)
        rows = [
            jnp.where(inside, jnp.where(lane == base + s, 1.0, 0.0), rows[s]) for s in range(TILE)
        ]
        for s in range(TILE):
            inverse = 1.0 / d[s][s]
            for i in range(TILE):
                if i == s:
                    continue
                factor = d[i][s] * inverse
                for j in range(s + 1, TILE):
                    d[i][j] = d[i][j] - factor * d[s][j]
                rows[i] = rows[i] - factor * rows[s]
            rows[s] = rows[s] * inverse
            for j in range(s + 1, TILE):
                d[s][j] = d[s][j] * inverse
        rows = [jnp.where(inside, -row, row) for row in rows]
        new = rows[0]
        for s in range(1, TILE):
            new = jnp.where(sub == s, rows[s], new)
        for k in range(1, count):
            i = (t + k) % count
            parts = [on_lanes(tiles[i], base + j) * rows[j] for j in range(TILE)]
            while len(parts) > 1:
                parts = [a + b for a, b in zip(parts[::2], parts[1::2])]
            tiles[i] = jnp.where(inside, 0.0, tiles[i]) - parts[0]
        tiles[t] = new
    return tiles


def block_inverse(block):
    tiles = negated_inverse([block[t * TILE : (t + 1) * TILE, :] for t in range(BLOCK // TILE)])
    return jnp.concatenate([-tile for tile in tiles], axis=0)


def with_diagonal(block, prior):
    row = lax.broadcasted_iota(jnp.int32, (BLOCK, BLOCK), 0)
    lane = lax.broadcasted_iota(jnp.int32, (BLOCK, BLOCK), 1)
    return block + jnp.where(row == lane, prior, 0.0)


def all_rows(ref, row):
    return jnp.broadcast_to(ref[row : row + 1, :], (TILE, BLOCK))


def packed_rows(lines):
    row = lax.broadcasted_iota(jnp.int32, (TILE, BLOCK), 0)
    out = jnp.zeros((TILE, BLOCK), f32)
    for k, line in enumerate(lines):
        out = jnp.where(row == k, line, out)
    return out


def factor_pairs(blocks):
    return {pair: n for n, pair in enumerate((k, i) for k in range(blocks) for i in range(k + 1, blocks))}


def mid_factor_kernel(place_ref, prior_ref, *refs):
    (*gram_refs, inverse_ref, factor_ref, held) = refs
    count, deep = len(gram_refs), gram_refs[0].shape[0]
    for d, ref in enumerate(gram_refs):
        at = lax.rem(place_ref[0] + (count - d), count)
        held[pl.ds(at * deep, deep), :, :] = ref[...]
    blocks = prior_ref.shape[1] // BLOCK
    tiles_each = held.shape[1] // TILE
    gram = {pair: load_block(held, n, tiles_each) for n, pair in enumerate(lower_blocks(blocks))}
    order = factor_pairs(blocks)
    for k in range(blocks):
        prior = prior_ref[:, k * BLOCK : (k + 1) * BLOCK]
        inverse = block_inverse(with_diagonal(gram[k, k], prior))
        inverse_ref[k * BLOCK : (k + 1) * BLOCK, :] = inverse
        for i in range(k + 1, blocks):
            factor = mm(gram[i, k], inverse)
            n = order[k, i]
            factor_ref[n * BLOCK : (n + 1) * BLOCK, :] = factor
            for j in range(k + 1, i + 1):
                gram[i, j] = gram[i, j] - mm_t(factor, gram[j, k])


def schur_kernel(deep, place_ref, inverse_ref, factor_ref, rhs_ref, *refs):
    (*cross_refs, out_ref, solved_ref, line_ref, root_ref, left, schur) = refs
    count = len(cross_refs)
    blocks = left.shape[0] // BLOCK
    fine = root_ref.shape[1]
    rows = cross_refs[0].shape[0] - fine
    slab = rows // deep
    strip = slab * BLOCK // left.shape[1]
    order = factor_pairs(blocks)
    for d, ref in enumerate(cross_refs):
        at = lax.rem(place_ref[0] + (count - d), count)
        start = pl.multiple_of(at * BLOCK, BLOCK)
        for j in range(left.shape[1] // BLOCK):
            left[pl.ds(start, BLOCK), j * BLOCK : (j + 1) * BLOCK] = jnp.concatenate(
                [
                    ref[z * slab + j * strip : z * slab + (j + 1) * strip, :]
                    for z in range(deep)
                ],
                axis=0,
            )
        root_ref[at] = ref[rows:, :]
    lines = [all_rows(rhs_ref, k) for k in range(blocks)]
    for i in range(blocks):
        own = slice(i * BLOCK, (i + 1) * BLOCK)
        if i > 0:
            row = jnp.concatenate(
                [factor_ref[order[k, i] * BLOCK : (order[k, i] + 1) * BLOCK, :] for k in range(i)],
                axis=1,
            )
            left[own, :] -= mm(row, left[: i * BLOCK, :])
            lines[i] = lines[i] - mm_t(jnp.concatenate(lines[:i], axis=1), row)
        solved_ref[own, :] = mm(inverse_ref[own, :], left[own, :])
    solved_lines = [
        mm(lines[k], inverse_ref[k * BLOCK : (k + 1) * BLOCK, :]) for k in range(blocks)
    ]
    for k in range(blocks):
        line_ref[k * TILE : (k + 1) * TILE, :] = solved_lines[k]
    for i in range(blocks):
        own = slice(i * BLOCK, (i + 1) * BLOCK)
        schur[own, : (i + 1) * BLOCK] = -t_mm(left[:, own], solved_ref[:, : (i + 1) * BLOCK])
    tiles_each = (out_ref.shape[1] - TILE) // TILE
    store_lower(schur, out_ref, tiles_each)
    moved = mm(jnp.concatenate(solved_lines, axis=1), left[...])
    packed = packed_rows(
        [
            all_rows(rhs_ref, blocks + k) - moved[:, k * BLOCK : (k + 1) * BLOCK]
            for k in range(blocks)
        ]
    )
    for g in range(out_ref.shape[0]):
        out_ref[g, tiles_each * TILE :, :] = packed


def back_kernel(solved_ref, factor_ref, line_ref, full_ref, vector_ref):
    blocks = solved_ref.shape[0] // BLOCK
    order = factor_pairs(blocks)
    for k in reversed(range(blocks)):
        own = slice(k * BLOCK, (k + 1) * BLOCK)
        full = solved_ref[own, :]
        line = line_ref[k * TILE : (k + 1) * TILE, :]
        if k + 1 < blocks:
            first, last = order[k, k + 1], order[k, blocks - 1]
            factor = factor_ref[first * BLOCK : (last + 1) * BLOCK, :]
            full = full - t_mm(factor, full_ref[(k + 1) * BLOCK :, :])
            line = line - mm(vector_ref[:, (k + 1) * BLOCK :], factor)
        full_ref[own, :] = full
        vector_ref[:, own] = line


def root_kernel(
    pieces, gram_ref, rhs_ref, prior_ref, full_ref, vector_ref, mid_ref, root_ref, root_out, mid_out, fit_ref, held_mid, held_root, sems_mid, sems_root
):
    copies_mid = start_copies(mid_ref, held_mid, sems_mid, pieces)
    copies_root = start_copies(root_ref, held_root, sems_root, pieces)
    blocks = prior_ref.shape[1] // BLOCK
    tiles_each = gram_ref.shape[1] // TILE
    gram = {pair: load_block(gram_ref, n, tiles_each) for n, pair in enumerate(lower_blocks(blocks))}
    lines = [all_rows(rhs_ref, k) for k in range(blocks)]
    factors = {}
    for k in range(blocks):
        prior = prior_ref[:, k * BLOCK : (k + 1) * BLOCK]
        inverse = block_inverse(with_diagonal(gram[k, k], prior))
        solved = mm(lines[k], inverse)
        for i in range(k + 1, blocks):
            factors[i, k] = mm(gram[i, k], inverse)
            for j in range(k + 1, i + 1):
                gram[i, j] = gram[i, j] - mm_t(factors[i, k], gram[j, k])
            lines[i] = lines[i] - mm_t(solved, gram[i, k])
        lines[k] = solved
    for k in reversed(range(blocks)):
        for i in range(k + 1, blocks):
            lines[k] = lines[k] - mm(lines[i], factors[i, k])
    means = jnp.concatenate(lines, axis=1)
    root_out[...] = means[:1, :]
    middle = vector_ref[...] - mm_t(means, full_ref[...])
    mid_out[...] = middle[:1, :]
    ones = jnp.ones((TILE, BLOCK), f32)
    each = held_mid.shape[0] // pieces
    for p in range(pieces):
        copies_mid[p].wait()
        copies_root[p].wait()
        for c in range(each // BLOCK):
            at = p * each + c * BLOCK
            total = 0.0
            for k in range(blocks):
                own = slice(k * BLOCK, (k + 1) * BLOCK)
                total = total + held_mid[at : at + BLOCK, own] * middle[:1, own]
                total = total + held_root[at : at + BLOCK, own] * means[:1, own]
            fit_ref[at // BLOCK : at // BLOCK + 1, :] = mm_t(ones, total)[:1, :]


def exchange(value, axis):
    return lax.all_to_all(value, axis, 0, 0, tiled=True)


def for_everyone(value, axis):
    return jnp.broadcast_to(value[None], (lax.axis_size(axis), *value.shape))


def moved_by(value, axis, step, stride, count):
    pairs = []
    for device in range(lax.axis_size(axis)):
        at = device // stride % count
        pairs.append((device, device + ((at + step) % count - at) * stride))
    return lax.ppermute(value, axis, pairs)


def swapped(value, axis, bit):
    return lax.ppermute(value, axis, [(d, d ^ bit) for d in range(lax.axis_size(axis))])


def part(value, index, dim=0):
    return lax.dynamic_index_in_dim(value, index, dim, keepdims=False)


def summed_over_line(value, axis, place, stride, count):
    total = part(value, place)
    sent = [
        moved_by(part(value, (place + d) & (count - 1)), axis, d, stride, count) for d in (1, count - 1, 2)
    ]
    for got in sent:
        total = total + got
    return total


def on_device(observed, noise_precision, mid_basis, root_basis, mid_prior, root_prior, leaf_count):
    slots, knots = mid_basis.shape
    root_knots = root_basis.shape[1]
    regions, groups = lax.axis_size("region"), lax.axis_size("group")
    deep, wide, cores = 8, regions // 8, 2
    region, group = lax.axis_index("region"), lax.axis_index("group")
    x, z = lax.div(region, deep), region & (deep - 1)
    y, core = lax.div(group, cores), group & 1
    chunks = slots // BLOCK
    noise = noise_precision.reshape(chunks, BLOCK)
    values = observed.reshape(chunks, BLOCK)
    blocks = knots // BLOCK
    packed = len(lower_blocks(blocks)) * BLOCK
    share = packed // regions
    group_share = packed // groups
    params = pltpu.CompilerParams(vmem_limit_bytes=VMEM_LIMIT)
    pieces = 4
    smem = pl.BlockSpec(memory_space=pltpu.SMEM)
    far = pl.BlockSpec(memory_space=pltpu.HBM)
    square = pltpu.VMEM((knots, knots), f32)
    rows = pltpu.VMEM((slots, knots), f32)
    waits = pltpu.SemaphoreType.DMA((pieces,))

    def cost(flops, size):
        return pl.CostEstimate(flops=int(flops), bytes_accessed=int(size), transcendentals=0)

    gram_flops = 2 * slots * knots * knots
    slab = knots // regions * (root_knots // BLOCK)
    parts, root_parts = pl.pallas_call(
        functools.partial(gram_kernel, pieces),
        out_shape=(
            jax.ShapeDtypeStruct((regions, TILE + share + slab, BLOCK), f32),
            jax.ShapeDtypeStruct((groups, group_share, BLOCK), f32),
        ),
        in_specs=[smem] + whole(2) + [far, far],
        out_specs=tuple(whole(2)),
        scratch_shapes=[
            rows,
            rows,
            pltpu.VMEM((knots, 2 * (knots + root_knots)), f32),
            square,
            pltpu.VMEM((root_knots, 2 * root_knots), f32),
            waits,
            waits,
        ],
        compiler_params=params,
        cost_estimate=cost(7 * gram_flops, 8 * slots * knots),
        name="gram",
    )(leaf_count, noise, values, mid_basis, root_basis)
    root_part = root_parts.reshape(groups // cores, cores, group_share, BLOCK)
    root_part = part(root_part, core, 1) + swapped(part(root_part, 1 - core, 1), "group", 1)
    root_part = summed_over_line(root_part, "group", y, cores, groups // cores)
    fine = group_share // wide
    root_part = summed_over_line(
        root_part.reshape(wide, fine, BLOCK), "region", x, deep, wide
    )
    parts = summed_over_line(
        parts.reshape(wide, deep, TILE + share + slab, BLOCK), "region", x, deep, wide
    )
    lines = [[a * deep + b for b in range(deep)] for a in range(wide)]

    def along_z(value):
        return lax.all_to_all(value, "region", 0, 0, tiled=True, axis_index_groups=lines)

    shares = along_z(parts).sum(axis=0)
    sent = jnp.concatenate([shares[TILE:], root_part])
    every_z = along_z(jnp.broadcast_to(sent[None], (deep, share + slab + fine, BLOCK)))

    def along_x(value):
        return [value] + [moved_by(value, "region", d, deep, wide) for d in range(1, wide)]

    mid_blocks = along_x(every_z[:, :share])
    cross_rows = every_z[:, share : share + slab].reshape(deep * slab, BLOCK)
    root_rows = every_z[:, share + slab :].sum(axis=0)
    cross_blocks = along_x(jnp.concatenate([cross_rows, root_rows]))

    pairs = blocks * (blocks - 1) // 2
    inverse, factor = pl.pallas_call(
        mid_factor_kernel,
        out_shape=(
            jax.ShapeDtypeStruct((knots, BLOCK), f32),
            jax.ShapeDtypeStruct((pairs * BLOCK, BLOCK), f32),
        ),
        in_specs=[smem] + whole(1 + wide),
        out_specs=tuple(whole(2)),
        scratch_shapes=[pltpu.VMEM((regions, share, BLOCK), f32)],
        compiler_params=params,
        cost_estimate=cost(2e10, 3e6),
        name="mid_factor",
    )(x.reshape(1), mid_prior, *mid_blocks)
    reduced, solved, line, root_pieces = pl.pallas_call(
        functools.partial(schur_kernel, deep),
        out_shape=(
            jax.ShapeDtypeStruct((groups, group_share + TILE, BLOCK), f32),
            jax.ShapeDtypeStruct((knots, root_knots), f32),
            jax.ShapeDtypeStruct((blocks * TILE, BLOCK), f32),
            jax.ShapeDtypeStruct((wide, fine, BLOCK), f32),
        ),
        in_specs=[smem] + whole(3 + wide),
        out_specs=tuple(whole(4)),
        scratch_shapes=[square, square],
        compiler_params=params,
        cost_estimate=cost(4e9, 4e6),
        name="schur",
    )(x.reshape(1), inverse, factor, shares[:TILE], *cross_blocks)
    root_part = root_pieces.reshape(group_share, BLOCK)
    full, vector = pl.pallas_call(
        back_kernel,
        out_shape=(
            jax.ShapeDtypeStruct((knots, root_knots), f32),
            jax.ShapeDtypeStruct((TILE, knots), f32),
        ),
        in_specs=whole(3),
        out_specs=tuple(whole(2)),
        compiler_params=params,
        cost_estimate=cost(4e9, 3e6),
        name="mid_back_substitution",
    )(solved, factor, line)

    summed = exchange(reduced, "group").sum(axis=0)
    root_all = exchange(for_everyone(summed[:group_share] + root_part, "group"), "group")

    root_means, mid_means, fit = pl.pallas_call(
        functools.partial(root_kernel, pieces),
        out_shape=(
            jax.ShapeDtypeStruct((1, root_knots), f32),
            jax.ShapeDtypeStruct((1, knots), f32),
            jax.ShapeDtypeStruct((chunks, BLOCK), f32),
        ),
        in_specs=whole(5) + [far, far],
        out_specs=tuple(whole(3)),
        scratch_shapes=[rows, rows, waits, waits],
        compiler_params=params,
        cost_estimate=cost(2.5e10, 8 * slots * knots),
        name="root_solve_and_fit",
    )(root_all, summed[group_share:], root_prior.reshape(1, root_knots), full, vector, mid_basis, root_basis)

    mid_slab = knots // regions
    middle = lax.dynamic_slice_in_dim(mid_means, region * mid_slab, mid_slab, 1)
    return root_means.reshape(root_knots), middle, fit.reshape(slots)


def solution(mesh):
    return jax.shard_map(
        on_device,
        mesh=mesh,
        in_specs=(
            P(("group", "region")),
            P(("group", "region")),
            P(("group", "region"), None),
            P(("group", "region"), None),
            P("group", None),
            P(),
            P("group", "region"),
        ),
        out_specs=(P(), P("group", "region"), P(("group", "region"))),
        check_vma=False,
    )
```

```python
import functools

import jax
import jax.numpy as jnp
from jax import lax
from jax.experimental import pallas as pl
from jax.experimental.pallas import tpu as pltpu
from jax.sharding import PartitionSpec as P

f32, bf16 = jnp.float32, jnp.bfloat16
BLOCK = 128
TILE = 8
VMEM_LIMIT = 56 * 1024 * 1024


def whole(count):
    return [pl.BlockSpec(memory_space=pltpu.VMEM)] * count


def lower_blocks(blocks):
    return [(i, j) for i in range(blocks) for j in range(i + 1)]


def product(a, b, dims):
    return lax.dot_general(
        a, b, (dims, ((), ())), precision=lax.Precision.HIGHEST, preferred_element_type=f32
    )


def mm(a, b):
    return product(a, b, ((1,), (0,)))


def mm_t(a, b):
    return product(a, b, ((1,), (1,)))


def t_mm(a, b):
    return product(a, b, ((0,), (0,)))


def halves(value):
    high = value.astype(bf16)
    return high, (value - high.astype(f32)).astype(bf16)


def bf_t_mm(a, b):
    return lax.dot_general(a, b, (((0,), (0,)), ((), ())), preferred_element_type=f32)


def weights_in_columns(count_ref, noise_ref, observed_ref):
    chunks = noise_ref.shape[0]
    slot = lax.broadcasted_iota(jnp.int32, (chunks, BLOCK), 0) * BLOCK + lax.broadcasted_iota(
        jnp.int32, (chunks, BLOCK), 1
    )
    weight = jnp.where(slot < count_ref[0, 0], noise_ref[...], 0.0)
    root = jnp.sqrt(weight)
    seen = root * observed_ref[...]
    stacked = jnp.concatenate([root, seen] * (BLOCK // (2 * chunks)), axis=0)
    turned = stacked.T
    return (
        [turned[:, c : c + 1] for c in range(chunks)],
        [turned[:, chunks + c : chunks + c + 1] for c in range(chunks)],
    )


def scaled_rows(rows_ref, start, columns, scaled_obs):
    rows, sums = [], 0.0
    for c, y in zip(columns, scaled_obs):
        part = rows_ref[start : start + BLOCK, :] * c
        sums = sums + jnp.sum((part * y).reshape(-1, TILE, part.shape[1]), axis=0)
        rows.append(part)
        start += BLOCK
    return jnp.concatenate(rows, axis=0), sums


def rows_of(vectors):
    row = lax.broadcasted_iota(jnp.int32, (TILE, BLOCK), 0)
    out, at = jnp.zeros((TILE, BLOCK), f32), 0
    for vector in vectors:
        line = jnp.sum(vector, axis=0, keepdims=True)
        for k in range(vector.shape[1] // BLOCK):
            out = jnp.where(row == at, line[:, k * BLOCK : (k + 1) * BLOCK], out)
            at += 1
    return out


def store_lower(matrix, out_ref, tiles_each, first=0):
    number = 0
    for i, j in lower_blocks(matrix.shape[0] // BLOCK):
        block = matrix[i * BLOCK : (i + 1) * BLOCK, j * BLOCK : (j + 1) * BLOCK]
        for t in range(BLOCK // TILE):
            at = first + TILE * (number % tiles_each)
            out_ref[number // tiles_each, at : at + TILE, :] = block[t * TILE : (t + 1) * TILE, :]
            number += 1


def load_tile(ref, block, t, tiles_each):
    number = block * (BLOCK // TILE) + t
    at = TILE * (number % tiles_each)
    return ref[number // tiles_each, at : at + TILE, :]


def load_block(ref, block, tiles_each):
    return jnp.concatenate(
        [load_tile(ref, block, t, tiles_each) for t in range(BLOCK // TILE)], axis=0
    )


def start_copies(source_ref, held_ref, sems, pieces):
    size = source_ref.shape[0] // pieces
    copies = []
    for p in range(pieces):
        copy = pltpu.make_async_copy(
            source_ref.at[pl.ds(p * size, size), :], held_ref.at[pl.ds(p * size, size), :], sems.at[p]
        )
        copy.start()
        copies.append(copy)
    return copies


def gram_kernel(
    pieces, count_ref, noise_ref, observed_ref, mid_prior_ref, root_prior_ref, mid_ref, root_ref, out_ref, root_out, mid_prior_out, root_prior_out, held_mid, held_root, by_mid, by_low, by_root, sems_mid, sems_root
):
    copies_mid = start_copies(mid_ref, held_mid, sems_mid, pieces)
    copies_root = start_copies(root_ref, held_root, sems_root, pieces)
    mid_prior_out[...] = mid_prior_ref[...]
    root_prior_out[...] = root_prior_ref[...]
    columns, scaled_obs = weights_in_columns(count_ref, noise_ref, observed_ref)
    each = len(columns) // pieces
    knots, root_knots = mid_ref.shape[1], root_ref.shape[1]
    mid_rhs, root_rhs = 0.0, 0.0
    for p in range(pieces):
        own = slice(p * each, (p + 1) * each)
        copies_mid[p].wait()
        mid_rows, mid_sums = scaled_rows(held_mid, p * each * BLOCK, columns[own], scaled_obs[own])
        copies_root[p].wait()
        root_rows, root_sums = scaled_rows(held_root, p * each * BLOCK, columns[own], scaled_obs[own])
        mid_rhs, root_rhs = mid_rhs + mid_sums, root_rhs + root_sums
        mid_high, mid_low = halves(mid_rows)
        root_high, root_low = halves(root_rows)
        root_both = jnp.concatenate([root_high, root_low], axis=1)
        products = (
            bf_t_mm(mid_high, jnp.concatenate([mid_high, mid_low, root_both], axis=1)),
            bf_t_mm(mid_low, root_high),
            bf_t_mm(root_high, root_both),
        )
        for ref, value in zip((by_mid, by_low, by_root), products):
            if p == 0:
                ref[...] = value
            else:
                ref[...] += value
    cross = by_mid[:, knots : 2 * knots]
    regions = out_ref.shape[0]
    slab = knots // regions
    cross_rows = slab * (root_knots // BLOCK)
    tiles_each = (out_ref.shape[1] - TILE - cross_rows) // TILE
    store_lower(by_mid[:, :knots] + (cross + cross.T), out_ref, tiles_each, TILE)
    line = rows_of([mid_rhs, root_rhs])
    for r in range(regions):
        out_ref[r, :TILE, :] = line
    first = TILE * (1 + tiles_each)
    for j in range(root_knots // BLOCK):
        own = slice(j * BLOCK, (j + 1) * BLOCK)
        high = by_mid[:, 2 * knots + j * BLOCK : 2 * knots + (j + 1) * BLOCK]
        low = by_mid[:, 2 * knots + root_knots + j * BLOCK : 2 * knots + root_knots + (j + 1) * BLOCK]
        block = high + (low + by_low[:, own])
        at = first + j * slab
        out_ref[:, at : at + slab, :] = block.reshape(regions, slab, BLOCK)
    cross = by_root[:, root_knots:]
    store_lower(by_root[:, :root_knots] + (cross + cross.T), root_out, root_out.shape[1] // TILE)


def on_lanes(tile, lane):
    return jnp.broadcast_to(tile[:, lane : lane + 1], (TILE, BLOCK))


def on_sublanes(tile, row):
    return jnp.broadcast_to(tile[row : row + 1, :], (TILE, BLOCK))


def negated_inverse(tiles):
    lane = lax.broadcasted_iota(jnp.int32, (TILE, BLOCK), 1)
    sub = lax.broadcasted_iota(jnp.int32, (TILE, BLOCK), 0)
    tiles = list(tiles)
    count = len(tiles)
    for t in range(count):
        base = TILE * t
        inside = (lane >= base) & (lane < base + TILE)
        columns = [on_lanes(tiles[t], base + j) for j in range(TILE)]
        new = jnp.where(inside, jnp.where(lane - base == sub, 1.0, 0.0), tiles[t])
        for s in range(TILE):
            pivot = sub == s
            inverse = 1.0 / on_sublanes(columns[s], s)
            factor = jnp.where(pivot, -1.0, columns[s])
            for j in range(s + 1, TILE):
                scaled = on_sublanes(columns[j], s) * inverse
                columns[j] = jnp.where(pivot, 0.0, columns[j]) - factor * scaled
            scaled = on_sublanes(new, s) * inverse
            new = jnp.where(pivot, 0.0, new) - factor * scaled
        new = jnp.where(inside, -new, new)
        rows = [on_sublanes(new, s) for s in range(TILE)]
        for k in range(1, count):
            i = (t + k) % count
            parts = [on_lanes(tiles[i], base + j) * rows[j] for j in range(TILE)]
            while len(parts) > 1:
                parts = [a + b for a, b in zip(parts[::2], parts[1::2])]
            tiles[i] = jnp.where(inside, 0.0, tiles[i]) - parts[0]
        tiles[t] = new
    return tiles


def block_inverse(block):
    tiles = negated_inverse([block[t * TILE : (t + 1) * TILE, :] for t in range(BLOCK // TILE)])
    return jnp.concatenate([-tile for tile in tiles], axis=0)


def with_diagonal(block, prior):
    row = lax.broadcasted_iota(jnp.int32, (BLOCK, BLOCK), 0)
    lane = lax.broadcasted_iota(jnp.int32, (BLOCK, BLOCK), 1)
    return block + jnp.where(row == lane, prior, 0.0)


def all_rows(ref, row):
    return jnp.broadcast_to(ref[row : row + 1, :], (TILE, BLOCK))


def packed_rows(lines):
    row = lax.broadcasted_iota(jnp.int32, (TILE, BLOCK), 0)
    out = jnp.zeros((TILE, BLOCK), f32)
    for k, line in enumerate(lines):
        out = jnp.where(row == k, line, out)
    return out


def factor_pairs(blocks):
    return {pair: n for n, pair in enumerate((k, i) for k in range(blocks) for i in range(k + 1, blocks))}


def mid_factor_kernel(place_ref, prior_ref, *refs):
    (*gram_refs, inverse_ref, factor_ref, held) = refs
    count, deep = len(gram_refs), gram_refs[0].shape[0]
    for d, ref in enumerate(gram_refs):
        at = lax.rem(place_ref[0] + (count - d), count)
        held[pl.ds(at * deep, deep), :, :] = ref[...]
    blocks = prior_ref.shape[1] // BLOCK
    tiles_each = held.shape[1] // TILE
    gram = {pair: load_block(held, n, tiles_each) for n, pair in enumerate(lower_blocks(blocks))}
    order = factor_pairs(blocks)
    for k in range(blocks):
        prior = prior_ref[:, k * BLOCK : (k + 1) * BLOCK]
        inverse = block_inverse(with_diagonal(gram[k, k], prior))
        inverse_ref[k * BLOCK : (k + 1) * BLOCK, :] = inverse
        for i in range(k + 1, blocks):
            factor = mm(gram[i, k], inverse)
            n = order[k, i]
            factor_ref[n * BLOCK : (n + 1) * BLOCK, :] = factor
            for j in range(k + 1, i + 1):
                gram[i, j] = gram[i, j] - mm_t(factor, gram[j, k])


def schur_kernel(deep, place_ref, inverse_ref, factor_ref, rhs_ref, *refs):
    (*cross_refs, out_ref, solved_ref, line_ref, root_ref, left, schur) = refs
    count = len(cross_refs)
    blocks = left.shape[0] // BLOCK
    fine = root_ref.shape[1]
    rows = cross_refs[0].shape[0] - fine
    slab = rows // deep
    strip = slab * BLOCK // left.shape[1]
    order = factor_pairs(blocks)
    for d, ref in enumerate(cross_refs):
        at = lax.rem(place_ref[0] + (count - d), count)
        start = pl.multiple_of(at * BLOCK, BLOCK)
        for j in range(left.shape[1] // BLOCK):
            left[pl.ds(start, BLOCK), j * BLOCK : (j + 1) * BLOCK] = jnp.concatenate(
                [
                    ref[z * slab + j * strip : z * slab + (j + 1) * strip, :]
                    for z in range(deep)
                ],
                axis=0,
            )
        root_ref[at] = ref[rows:, :]
    lines = [all_rows(rhs_ref, k) for k in range(blocks)]
    for i in range(blocks):
        own = slice(i * BLOCK, (i + 1) * BLOCK)
        if i > 0:
            row = jnp.concatenate(
                [factor_ref[order[k, i] * BLOCK : (order[k, i] + 1) * BLOCK, :] for k in range(i)],
                axis=1,
            )
            left[own, :] -= mm(row, left[: i * BLOCK, :])
            lines[i] = lines[i] - mm_t(jnp.concatenate(lines[:i], axis=1), row)
        solved_ref[own, :] = mm(inverse_ref[own, :], left[own, :])
    solved_lines = [
        mm(lines[k], inverse_ref[k * BLOCK : (k + 1) * BLOCK, :]) for k in range(blocks)
    ]
    for k in range(blocks):
        line_ref[k * TILE : (k + 1) * TILE, :] = solved_lines[k]
    for i in range(blocks):
        own = slice(i * BLOCK, (i + 1) * BLOCK)
        schur[own, : (i + 1) * BLOCK] = -t_mm(left[:, own], solved_ref[:, : (i + 1) * BLOCK])
    tiles_each = (out_ref.shape[1] - TILE) // TILE
    store_lower(schur, out_ref, tiles_each)
    moved = mm(jnp.concatenate(solved_lines, axis=1), left[...])
    packed = packed_rows(
        [
            all_rows(rhs_ref, blocks + k) - moved[:, k * BLOCK : (k + 1) * BLOCK]
            for k in range(blocks)
        ]
    )
    for g in range(out_ref.shape[0]):
        out_ref[g, tiles_each * TILE :, :] = packed


def back_kernel(solved_ref, factor_ref, line_ref, full_ref, vector_ref):
    blocks = solved_ref.shape[0] // BLOCK
    order = factor_pairs(blocks)
    for k in reversed(range(blocks)):
        own = slice(k * BLOCK, (k + 1) * BLOCK)
        full = solved_ref[own, :]
        line = line_ref[k * TILE : (k + 1) * TILE, :]
        if k + 1 < blocks:
            first, last = order[k, k + 1], order[k, blocks - 1]
            factor = factor_ref[first * BLOCK : (last + 1) * BLOCK, :]
            full = full - t_mm(factor, full_ref[(k + 1) * BLOCK :, :])
            line = line - mm(vector_ref[:, (k + 1) * BLOCK :], factor)
        full_ref[own, :] = full
        vector_ref[:, own] = line


def root_kernel(
    pieces, gram_ref, rhs_ref, prior_ref, full_ref, vector_ref, mid_ref, root_ref, root_out, mid_out, fit_ref, held_mid, held_root, sems_mid, sems_root
):
    copies_mid = start_copies(mid_ref, held_mid, sems_mid, pieces)
    copies_root = start_copies(root_ref, held_root, sems_root, pieces)
    blocks = prior_ref.shape[1] // BLOCK
    tiles_each = gram_ref.shape[1] // TILE
    gram = {pair: load_block(gram_ref, n, tiles_each) for n, pair in enumerate(lower_blocks(blocks))}
    lines = [all_rows(rhs_ref, k) for k in range(blocks)]
    factors = {}
    for k in range(blocks):
        prior = prior_ref[:, k * BLOCK : (k + 1) * BLOCK]
        inverse = block_inverse(with_diagonal(gram[k, k], prior))
        solved = mm(lines[k], inverse)
        for i in range(k + 1, blocks):
            factors[i, k] = mm(gram[i, k], inverse)
            for j in range(k + 1, i + 1):
                gram[i, j] = gram[i, j] - mm_t(factors[i, k], gram[j, k])
            lines[i] = lines[i] - mm_t(solved, gram[i, k])
        lines[k] = solved
    for k in reversed(range(blocks)):
        for i in range(k + 1, blocks):
            lines[k] = lines[k] - mm(lines[i], factors[i, k])
    means = jnp.concatenate(lines, axis=1)
    root_out[...] = means[:1, :]
    middle = vector_ref[...] - mm_t(means, full_ref[...])
    mid_out[...] = middle[:1, :]
    ones = jnp.ones((TILE, BLOCK), f32)
    each = held_mid.shape[0] // pieces
    for p in range(pieces):
        copies_mid[p].wait()
        copies_root[p].wait()
        for c in range(each // BLOCK):
            at = p * each + c * BLOCK
            total = 0.0
            for k in range(blocks):
                own = slice(k * BLOCK, (k + 1) * BLOCK)
                total = total + held_mid[at : at + BLOCK, own] * middle[:1, own]
                total = total + held_root[at : at + BLOCK, own] * means[:1, own]
            fit_ref[at // BLOCK : at // BLOCK + 1, :] = mm_t(ones, total)[:1, :]


def exchange(value, axis):
    return lax.all_to_all(value, axis, 0, 0, tiled=True)


def for_everyone(value, axis):
    return jnp.broadcast_to(value[None], (lax.axis_size(axis), *value.shape))


def moved_by(value, axis, step, stride, count):
    pairs = []
    for device in range(lax.axis_size(axis)):
        at = device // stride % count
        pairs.append((device, device + ((at + step) % count - at) * stride))
    return lax.ppermute(value, axis, pairs)


def swapped(value, axis, bit):
    return lax.ppermute(value, axis, [(d, d ^ bit) for d in range(lax.axis_size(axis))])


def part(value, index, dim=0):
    return lax.dynamic_index_in_dim(value, index, dim, keepdims=False)


def summed_over_line(value, axis, place, stride, count):
    total = part(value, place)
    sent = [
        moved_by(part(value, (place + d) & (count - 1)), axis, d, stride, count) for d in (1, count - 1, 2)
    ]
    for got in sent:
        total = total + got
    return total


def summed_around(value, axis, place, stride):
    count, half = value.shape[0], value.shape[1] // 2

    def moved(sent, step):
        return moved_by(sent, axis, step, stride, count)

    own, up, far, down = (part(value, (place + d) & (count - 1)) for d in range(count))
    far_up, far_down = moved(far[:half], 1), moved(far[half:], -1)
    up_last, down_first = moved(up[half:], 1), moved(down[:half], -1)
    up_first = moved(up[:half] + far_up, 1)
    down_last = moved(down[half:] + far_down, -1)
    return jnp.concatenate([own[:half] + down_first + up_first, own[half:] + up_last + down_last])


def on_device(observed, noise_precision, mid_basis, root_basis, mid_prior, root_prior, leaf_count):
    slots, knots = mid_basis.shape
    root_knots = root_basis.shape[1]
    regions, groups = lax.axis_size("region"), lax.axis_size("group")
    deep, wide, cores = 8, regions // 8, 2
    region, group = lax.axis_index("region"), lax.axis_index("group")
    x, z = lax.div(region, deep), region & (deep - 1)
    y, core = lax.div(group, cores), group & 1
    chunks = slots // BLOCK
    noise = noise_precision.reshape(chunks, BLOCK)
    values = observed.reshape(chunks, BLOCK)
    blocks = knots // BLOCK
    packed = len(lower_blocks(blocks)) * BLOCK
    share = packed // regions
    group_share = packed // groups
    params = pltpu.CompilerParams(vmem_limit_bytes=VMEM_LIMIT)
    pieces = 4
    smem = pl.BlockSpec(memory_space=pltpu.SMEM)
    far = pl.BlockSpec(memory_space=pltpu.HBM)
    square = pltpu.VMEM((knots, knots), f32)
    rows = pltpu.VMEM((slots, knots), f32)
    waits = pltpu.SemaphoreType.DMA((pieces,))

    def cost(flops, size):
        return pl.CostEstimate(flops=int(flops), bytes_accessed=int(size), transcendentals=0)

    gram_flops = 2 * slots * knots * knots
    slab = knots // regions * (root_knots // BLOCK)
    parts, root_parts, mid_diagonal, root_diagonal = pl.pallas_call(
        functools.partial(gram_kernel, pieces),
        out_shape=(
            jax.ShapeDtypeStruct((regions, TILE + share + slab, BLOCK), f32),
            jax.ShapeDtypeStruct((groups, group_share, BLOCK), f32),
            jax.ShapeDtypeStruct((1, knots), f32),
            jax.ShapeDtypeStruct((1, root_knots), f32),
        ),
        in_specs=[smem] + whole(4) + [far, far],
        out_specs=tuple(whole(4)),
        scratch_shapes=[
            rows,
            rows,
            pltpu.VMEM((knots, 2 * (knots + root_knots)), f32),
            square,
            pltpu.VMEM((root_knots, 2 * root_knots), f32),
            waits,
            waits,
        ],
        compiler_params=params,
        cost_estimate=cost(7 * gram_flops, 8 * slots * knots),
        name="gram",
    )(leaf_count, noise, values, mid_prior, root_prior.reshape(1, root_knots), mid_basis, root_basis)
    root_part = root_parts.reshape(groups // cores, cores, group_share, BLOCK)
    root_part = part(root_part, core, 1) + swapped(part(root_part, 1 - core, 1), "group", 1)
    root_part = summed_over_line(root_part, "group", y, cores, groups // cores)
    fine = group_share // wide
    root_part = summed_over_line(
        root_part.reshape(wide, fine, BLOCK), "region", x, deep, wide
    )
    parts = summed_around(parts.reshape(wide, deep, TILE + share + slab, BLOCK), "region", x, deep)
    lines = [[a * deep + b for b in range(deep)] for a in range(wide)]

    def along_z(value):
        return lax.all_to_all(value, "region", 0, 0, tiled=True, axis_index_groups=lines)

    shares = along_z(parts).sum(axis=0)
    sent = jnp.concatenate([shares[TILE:], root_part])
    every_z = along_z(jnp.broadcast_to(sent[None], (deep, share + slab + fine, BLOCK)))

    def along_x(value):
        return [value] + [moved_by(value, "region", d, deep, wide) for d in range(1, wide)]

    mid_blocks = along_x(every_z[:, :share])
    cross_rows = every_z[:, share : share + slab].reshape(deep * slab, BLOCK)
    root_rows = every_z[:, share + slab :].sum(axis=0)
    cross_blocks = along_x(jnp.concatenate([cross_rows, root_rows]))

    pairs = blocks * (blocks - 1) // 2
    inverse, factor = pl.pallas_call(
        mid_factor_kernel,
        out_shape=(
            jax.ShapeDtypeStruct((knots, BLOCK), f32),
            jax.ShapeDtypeStruct((pairs * BLOCK, BLOCK), f32),
        ),
        in_specs=[smem] + whole(1 + wide),
        out_specs=tuple(whole(2)),
        scratch_shapes=[pltpu.VMEM((regions, share, BLOCK), f32)],
        compiler_params=params,
        cost_estimate=cost(2e10, 3e6),
        name="mid_factor",
    )(x.reshape(1), mid_diagonal, *mid_blocks)
    reduced, solved, line, root_pieces = pl.pallas_call(
        functools.partial(schur_kernel, deep),
        out_shape=(
            jax.ShapeDtypeStruct((groups, group_share + TILE, BLOCK), f32),
            jax.ShapeDtypeStruct((knots, root_knots), f32),
            jax.ShapeDtypeStruct((blocks * TILE, BLOCK), f32),
            jax.ShapeDtypeStruct((wide, fine, BLOCK), f32),
        ),
        in_specs=[smem] + whole(3 + wide),
        out_specs=tuple(whole(4)),
        scratch_shapes=[square, square],
        compiler_params=params,
        cost_estimate=cost(4e9, 4e6),
        name="schur",
    )(x.reshape(1), inverse, factor, shares[:TILE], *cross_blocks)
    root_part = root_pieces.reshape(group_share, BLOCK)
    full, vector = pl.pallas_call(
        back_kernel,
        out_shape=(
            jax.ShapeDtypeStruct((knots, root_knots), f32),
            jax.ShapeDtypeStruct((TILE, knots), f32),
        ),
        in_specs=whole(3),
        out_specs=tuple(whole(2)),
        compiler_params=params,
        cost_estimate=cost(4e9, 3e6),
        name="mid_back_substitution",
    )(solved, factor, line)

    summed = exchange(reduced, "group").sum(axis=0)
    root_all = exchange(for_everyone(summed[:group_share] + root_part, "group"), "group")

    root_means, mid_means, fit = pl.pallas_call(
        functools.partial(root_kernel, pieces),
        out_shape=(
            jax.ShapeDtypeStruct((1, root_knots), f32),
            jax.ShapeDtypeStruct((1, knots), f32),
            jax.ShapeDtypeStruct((chunks, BLOCK), f32),
        ),
        in_specs=whole(5) + [far, far],
        out_specs=tuple(whole(3)),
        scratch_shapes=[rows, rows, waits, waits],
        compiler_params=params,
        cost_estimate=cost(2.5e10, 8 * slots * knots),
        name="root_solve_and_fit",
    )(root_all, summed[group_share:], root_diagonal, full, vector, mid_basis, root_basis)

    mid_slab = knots // regions
    middle = lax.dynamic_slice_in_dim(mid_means, region * mid_slab, mid_slab, 1)
    return root_means.reshape(root_knots), middle, fit.reshape(slots)


def solution(mesh):
    return jax.shard_map(
        on_device,
        mesh=mesh,
        in_specs=(
            P(("group", "region")),
            P(("group", "region")),
            P(("group", "region"), None),
            P(("group", "region"), None),
            P("group", None),
            P(),
            P("group", "region"),
        ),
        out_specs=(P(), P("group", "region"), P(("group", "region"))),
        check_vma=False,
    )
```

```python
import functools

import jax
import jax.numpy as jnp
from jax import lax
from jax.experimental import pallas as pl
from jax.experimental.pallas import tpu as pltpu
from jax.sharding import PartitionSpec as P

f32, bf16 = jnp.float32, jnp.bfloat16
BLOCK = 128
TILE = 8
VMEM_LIMIT = 56 * 1024 * 1024


def whole(count):
    return [pl.BlockSpec(memory_space=pltpu.VMEM)] * count


def lower_blocks(blocks):
    return [(i, j) for i in range(blocks) for j in range(i + 1)]


def product(a, b, dims):
    return lax.dot_general(
        a, b, (dims, ((), ())), precision=lax.Precision.HIGHEST, preferred_element_type=f32
    )


def mm(a, b):
    return product(a, b, ((1,), (0,)))


def mm_t(a, b):
    return product(a, b, ((1,), (1,)))


def t_mm(a, b):
    return product(a, b, ((0,), (0,)))


def mm_t_by_halves(a, b):
    (a_high, a_low), (b_high, b_low) = halves(a), halves(b)

    def one(u, v):
        return lax.dot_general(u, v, (((1,), (1,)), ((), ())), preferred_element_type=f32)

    return one(a_high, b_high) + (one(a_high, b_low) + one(a_low, b_high))


def row_sums(value):
    ones = jnp.ones((TILE, value.shape[1]), bf16)
    return sum(
        lax.dot_general(ones, v, (((1,), (1,)), ((), ())), preferred_element_type=f32)
        for v in halves(value)
    )[:1, :]


def halves(value):
    high = value.astype(bf16)
    return high, (value - high.astype(f32)).astype(bf16)


def bf_t_mm(a, b):
    return lax.dot_general(a, b, (((0,), (0,)), ((), ())), preferred_element_type=f32)


def weights_in_columns(count_ref, noise_ref, observed_ref):
    chunks = noise_ref.shape[0]
    slot = lax.broadcasted_iota(jnp.int32, (chunks, BLOCK), 0) * BLOCK + lax.broadcasted_iota(
        jnp.int32, (chunks, BLOCK), 1
    )
    weight = jnp.where(slot < count_ref[0, 0], noise_ref[...], 0.0)
    root = jnp.sqrt(weight)
    seen = root * observed_ref[...]
    stacked = jnp.concatenate([root, seen] * (BLOCK // (2 * chunks)), axis=0)
    turned = stacked.T
    return (
        [turned[:, c : c + 1] for c in range(chunks)],
        [turned[:, chunks + c : chunks + c + 1] for c in range(chunks)],
    )


def scaled_rows(rows_ref, start, columns, scaled_obs):
    rows, sums = [], 0.0
    for c, y in zip(columns, scaled_obs):
        part = rows_ref[start : start + BLOCK, :] * c
        sums = sums + jnp.sum((part * y).reshape(-1, TILE, part.shape[1]), axis=0)
        rows.append(part)
        start += BLOCK
    return jnp.concatenate(rows, axis=0), sums


def rows_of(vectors):
    row = lax.broadcasted_iota(jnp.int32, (TILE, BLOCK), 0)
    out, at = jnp.zeros((TILE, BLOCK), f32), 0
    for vector in vectors:
        line = jnp.sum(vector, axis=0, keepdims=True)
        for k in range(vector.shape[1] // BLOCK):
            out = jnp.where(row == at, line[:, k * BLOCK : (k + 1) * BLOCK], out)
            at += 1
    return out


def store_lower(matrix, out_ref, tiles_each, first=0):
    number = 0
    for i, j in lower_blocks(matrix.shape[0] // BLOCK):
        block = matrix[i * BLOCK : (i + 1) * BLOCK, j * BLOCK : (j + 1) * BLOCK]
        for t in range(BLOCK // TILE):
            at = first + TILE * (number % tiles_each)
            out_ref[number // tiles_each, at : at + TILE, :] = block[t * TILE : (t + 1) * TILE, :]
            number += 1


def load_tile(ref, block, t, tiles_each):
    number = block * (BLOCK // TILE) + t
    at = TILE * (number % tiles_each)
    return ref[number // tiles_each, at : at + TILE, :]


def load_block(ref, block, tiles_each):
    return jnp.concatenate(
        [load_tile(ref, block, t, tiles_each) for t in range(BLOCK // TILE)], axis=0
    )


def start_copies(source_ref, held_ref, sems, pieces):
    size = source_ref.shape[0] // pieces
    copies = []
    for p in range(pieces):
        copy = pltpu.make_async_copy(
            source_ref.at[pl.ds(p * size, size), :], held_ref.at[pl.ds(p * size, size), :], sems.at[p]
        )
        copy.start()
        copies.append(copy)
    return copies


def gram_kernel(
    pieces, place_ref, count_ref, noise_ref, observed_ref, mid_prior_ref, root_prior_ref, mid_ref, root_ref, own_out, up_first, up_last, far_first, far_last, down_first, down_last, root_out, mid_prior_out, root_prior_out, out_ref, held_mid, held_root, by_mid, by_low, by_root, sems_mid, sems_root
):
    copies_mid = start_copies(mid_ref, held_mid, sems_mid, pieces)
    copies_root = start_copies(root_ref, held_root, sems_root, pieces)
    mid_prior_out[...] = mid_prior_ref[...]
    root_prior_out[...] = root_prior_ref[...]
    columns, scaled_obs = weights_in_columns(count_ref, noise_ref, observed_ref)
    each = len(columns) // pieces
    knots, root_knots = mid_ref.shape[1], root_ref.shape[1]
    mid_rhs, root_rhs = 0.0, 0.0
    for p in range(pieces):
        own = slice(p * each, (p + 1) * each)
        copies_mid[p].wait()
        mid_rows, mid_sums = scaled_rows(held_mid, p * each * BLOCK, columns[own], scaled_obs[own])
        copies_root[p].wait()
        root_rows, root_sums = scaled_rows(held_root, p * each * BLOCK, columns[own], scaled_obs[own])
        mid_rhs, root_rhs = mid_rhs + mid_sums, root_rhs + root_sums
        mid_high, mid_low = halves(mid_rows)
        root_high, root_low = halves(root_rows)
        root_both = jnp.concatenate([root_high, root_low], axis=1)
        products = (
            bf_t_mm(mid_high, jnp.concatenate([mid_high, mid_low, root_both], axis=1)),
            bf_t_mm(mid_low, root_high),
            bf_t_mm(root_high, root_both),
        )
        for ref, value in zip((by_mid, by_low, by_root), products):
            if p == 0:
                ref[...] = value
            else:
                ref[...] += value
    cross = by_mid[:, knots : 2 * knots]
    regions = out_ref.shape[0]
    slab = knots // regions
    cross_rows = slab * (root_knots // BLOCK)
    tiles_each = (out_ref.shape[1] - TILE - cross_rows) // TILE
    store_lower(by_mid[:, :knots] + (cross + cross.T), out_ref, tiles_each, TILE)
    line = rows_of([mid_rhs, root_rhs])
    for r in range(regions):
        out_ref[r, :TILE, :] = line
    first = TILE * (1 + tiles_each)
    for j in range(root_knots // BLOCK):
        own = slice(j * BLOCK, (j + 1) * BLOCK)
        high = by_mid[:, 2 * knots + j * BLOCK : 2 * knots + (j + 1) * BLOCK]
        low = by_mid[:, 2 * knots + root_knots + j * BLOCK : 2 * knots + root_knots + (j + 1) * BLOCK]
        block = high + (low + by_low[:, own])
        at = first + j * slab
        out_ref[:, at : at + slab, :] = block.reshape(regions, slab, BLOCK)
    deep, half = own_out.shape[0], up_first.shape[0]
    wide = regions // deep
    own_out[...] = out_ref[pl.ds(place_ref[0] * deep, deep), :, :]
    for d, (first, last) in enumerate(
        ((up_first, up_last), (far_first, far_last), (down_first, down_last)), 1
    ):
        start = lax.rem(place_ref[0] + d, wide) * deep
        first[...] = out_ref[pl.ds(start, half), :, :]
        last[...] = out_ref[pl.ds(start + half, deep - half), :, :]
    cross = by_root[:, root_knots:]
    store_lower(by_root[:, :root_knots] + (cross + cross.T), root_out, root_out.shape[1] // TILE)


def on_lanes(tile, lane):
    return jnp.broadcast_to(tile[:, lane : lane + 1], (TILE, BLOCK))


def on_sublanes(tile, row):
    return jnp.broadcast_to(tile[row : row + 1, :], (TILE, BLOCK))


def negated_inverse(tiles):
    lane = lax.broadcasted_iota(jnp.int32, (TILE, BLOCK), 1)
    sub = lax.broadcasted_iota(jnp.int32, (TILE, BLOCK), 0)
    tiles = list(tiles)
    count = len(tiles)
    for t in range(count):
        base = TILE * t
        inside = (lane >= base) & (lane < base + TILE)
        columns = [on_lanes(tiles[t], base + j) for j in range(TILE)]
        new = jnp.where(inside, jnp.where(lane - base == sub, 1.0, 0.0), tiles[t])
        for s in range(TILE):
            pivot = sub == s
            inverse = 1.0 / on_sublanes(columns[s], s)
            factor = jnp.where(pivot, -1.0, columns[s])
            for j in range(s + 1, TILE):
                scaled = on_sublanes(columns[j], s) * inverse
                columns[j] = jnp.where(pivot, 0.0, columns[j]) - factor * scaled
            scaled = on_sublanes(new, s) * inverse
            new = jnp.where(pivot, 0.0, new) - factor * scaled
        new = jnp.where(inside, -new, new)
        rows = [on_sublanes(new, s) for s in range(TILE)]
        for k in range(1, count):
            i = (t + k) % count
            parts = [on_lanes(tiles[i], base + j) * rows[j] for j in range(TILE)]
            while len(parts) > 1:
                parts = [a + b for a, b in zip(parts[::2], parts[1::2])]
            tiles[i] = jnp.where(inside, 0.0, tiles[i]) - parts[0]
        tiles[t] = new
    return tiles


def block_inverse(block):
    tiles = negated_inverse([block[t * TILE : (t + 1) * TILE, :] for t in range(BLOCK // TILE)])
    return jnp.concatenate([-tile for tile in tiles], axis=0)


def with_diagonal(block, prior):
    row = lax.broadcasted_iota(jnp.int32, (BLOCK, BLOCK), 0)
    lane = lax.broadcasted_iota(jnp.int32, (BLOCK, BLOCK), 1)
    return block + jnp.where(row == lane, prior, 0.0)


def all_rows(ref, row):
    return jnp.broadcast_to(ref[row : row + 1, :], (TILE, BLOCK))


def packed_rows(lines):
    row = lax.broadcasted_iota(jnp.int32, (TILE, BLOCK), 0)
    out = jnp.zeros((TILE, BLOCK), f32)
    for k, line in enumerate(lines):
        out = jnp.where(row == k, line, out)
    return out


def factor_pairs(blocks):
    return {pair: n for n, pair in enumerate((k, i) for k in range(blocks) for i in range(k + 1, blocks))}


def mid_factor_kernel(place_ref, prior_ref, *refs):
    (*gram_refs, inverse_ref, factor_ref, held) = refs
    count, deep = len(gram_refs), gram_refs[0].shape[0]
    for d, ref in enumerate(gram_refs):
        at = lax.rem(place_ref[0] + (count - d), count)
        held[pl.ds(at * deep, deep), :, :] = ref[...]
    blocks = prior_ref.shape[1] // BLOCK
    tiles_each = held.shape[1] // TILE
    gram = {pair: load_block(held, n, tiles_each) for n, pair in enumerate(lower_blocks(blocks))}
    order = factor_pairs(blocks)
    for k in range(blocks):
        prior = prior_ref[:, k * BLOCK : (k + 1) * BLOCK]
        inverse = block_inverse(with_diagonal(gram[k, k], prior))
        inverse_ref[k * BLOCK : (k + 1) * BLOCK, :] = inverse
        for i in range(k + 1, blocks):
            factor = mm(gram[i, k], inverse)
            n = order[k, i]
            factor_ref[n * BLOCK : (n + 1) * BLOCK, :] = factor
            for j in range(k + 1, i + 1):
                gram[i, j] = gram[i, j] - mm_t(factor, gram[j, k])


def schur_kernel(deep, place_ref, inverse_ref, factor_ref, rhs_ref, *refs):
    (*cross_refs, out_ref, solved_ref, line_ref, root_ref, left, schur) = refs
    count = len(cross_refs)
    blocks = left.shape[0] // BLOCK
    fine = root_ref.shape[1]
    rows = cross_refs[0].shape[0] - fine
    slab = rows // deep
    strip = slab * BLOCK // left.shape[1]
    order = factor_pairs(blocks)
    for d, ref in enumerate(cross_refs):
        at = lax.rem(place_ref[0] + (count - d), count)
        start = pl.multiple_of(at * BLOCK, BLOCK)
        for j in range(left.shape[1] // BLOCK):
            left[pl.ds(start, BLOCK), j * BLOCK : (j + 1) * BLOCK] = jnp.concatenate(
                [
                    ref[z * slab + j * strip : z * slab + (j + 1) * strip, :]
                    for z in range(deep)
                ],
                axis=0,
            )
        root_ref[at] = ref[rows:, :]
    lines = [all_rows(rhs_ref, k) for k in range(blocks)]
    for i in range(blocks):
        own = slice(i * BLOCK, (i + 1) * BLOCK)
        if i > 0:
            row = jnp.concatenate(
                [factor_ref[order[k, i] * BLOCK : (order[k, i] + 1) * BLOCK, :] for k in range(i)],
                axis=1,
            )
            left[own, :] -= mm(row, left[: i * BLOCK, :])
            lines[i] = lines[i] - mm_t(jnp.concatenate(lines[:i], axis=1), row)
        solved_ref[own, :] = mm(inverse_ref[own, :], left[own, :])
    solved_lines = [
        mm(lines[k], inverse_ref[k * BLOCK : (k + 1) * BLOCK, :]) for k in range(blocks)
    ]
    for k in range(blocks):
        line_ref[k * TILE : (k + 1) * TILE, :] = solved_lines[k]
    for i in range(blocks):
        own = slice(i * BLOCK, (i + 1) * BLOCK)
        schur[own, : (i + 1) * BLOCK] = -t_mm(left[:, own], solved_ref[:, : (i + 1) * BLOCK])
    tiles_each = (out_ref.shape[1] - TILE) // TILE
    store_lower(schur, out_ref, tiles_each)
    moved = mm(jnp.concatenate(solved_lines, axis=1), left[...])
    packed = packed_rows(
        [
            all_rows(rhs_ref, blocks + k) - moved[:, k * BLOCK : (k + 1) * BLOCK]
            for k in range(blocks)
        ]
    )
    for g in range(out_ref.shape[0]):
        out_ref[g, tiles_each * TILE :, :] = packed


def back_kernel(solved_ref, factor_ref, line_ref, full_ref, vector_ref):
    blocks = solved_ref.shape[0] // BLOCK
    order = factor_pairs(blocks)
    for k in reversed(range(blocks)):
        own = slice(k * BLOCK, (k + 1) * BLOCK)
        full = solved_ref[own, :]
        line = line_ref[k * TILE : (k + 1) * TILE, :]
        if k + 1 < blocks:
            first, last = order[k, k + 1], order[k, blocks - 1]
            factor = factor_ref[first * BLOCK : (last + 1) * BLOCK, :]
            full = full - t_mm(factor, full_ref[(k + 1) * BLOCK :, :])
            line = line - mm(vector_ref[:, (k + 1) * BLOCK :], factor)
        full_ref[own, :] = full
        vector_ref[:, own] = line


def root_kernel(
    pieces, gram_ref, rhs_ref, prior_ref, full_ref, vector_ref, mid_ref, root_ref, root_out, mid_out, fit_ref, held_mid, held_root, sems_mid, sems_root
):
    copies_mid = start_copies(mid_ref, held_mid, sems_mid, pieces)
    copies_root = start_copies(root_ref, held_root, sems_root, pieces)
    blocks = prior_ref.shape[1] // BLOCK
    tiles_each = gram_ref.shape[1] // TILE
    gram = {pair: load_block(gram_ref, n, tiles_each) for n, pair in enumerate(lower_blocks(blocks))}
    lines = [all_rows(rhs_ref, k) for k in range(blocks)]
    factors = {}
    for k in range(blocks):
        prior = prior_ref[:, k * BLOCK : (k + 1) * BLOCK]
        inverse = block_inverse(with_diagonal(gram[k, k], prior))
        solved = mm(lines[k], inverse)
        for i in range(k + 1, blocks):
            factors[i, k] = mm(gram[i, k], inverse)
            for j in range(k + 1, i + 1):
                gram[i, j] = gram[i, j] - mm_t(factors[i, k], gram[j, k])
            lines[i] = lines[i] - mm_t(solved, gram[i, k])
        lines[k] = solved
    for k in reversed(range(blocks)):
        for i in range(k + 1, blocks):
            lines[k] = lines[k] - mm(lines[i], factors[i, k])
    means = jnp.concatenate(lines, axis=1)
    root_out[...] = means[:1, :]
    middle = vector_ref[...] - mm_t_by_halves(means, full_ref[...])
    mid_out[...] = middle[:1, :]
    each = held_mid.shape[0] // pieces
    for p in range(pieces):
        copies_mid[p].wait()
        copies_root[p].wait()
        for c in range(each // BLOCK):
            at = p * each + c * BLOCK
            total = 0.0
            for k in range(blocks):
                own = slice(k * BLOCK, (k + 1) * BLOCK)
                total = total + held_mid[at : at + BLOCK, own] * middle[:1, own]
                total = total + held_root[at : at + BLOCK, own] * means[:1, own]
            fit_ref[at // BLOCK : at // BLOCK + 1, :] = row_sums(total)


def exchange(value, axis):
    return lax.all_to_all(value, axis, 0, 0, tiled=True)


def for_everyone(value, axis):
    return jnp.broadcast_to(value[None], (lax.axis_size(axis), *value.shape))


def moved_by(value, axis, step, stride, count):
    pairs = []
    for device in range(lax.axis_size(axis)):
        at = device // stride % count
        pairs.append((device, device + ((at + step) % count - at) * stride))
    return lax.ppermute(value, axis, pairs)


def swapped(value, axis, bit):
    return lax.ppermute(value, axis, [(d, d ^ bit) for d in range(lax.axis_size(axis))])


def part(value, index, dim=0):
    return lax.dynamic_index_in_dim(value, index, dim, keepdims=False)


def summed_over_line(value, axis, place, stride, count):
    total = part(value, place)
    sent = [
        moved_by(part(value, (place + d) & (count - 1)), axis, d, stride, count) for d in (1, count - 1, 2)
    ]
    for got in sent:
        total = total + got
    return total


def summed_around(own, up, far, down, axis, stride, count):
    def moved(sent, step):
        return moved_by(sent, axis, step, stride, count)

    far_up, far_down = moved(far[0], 1), moved(far[1], -1)
    up_last, down_first = moved(up[1], 1), moved(down[0], -1)
    up_first = moved(up[0] + far_up, 1)
    down_last = moved(down[1] + far_down, -1)
    half = far[0].shape[0]
    return jnp.concatenate([own[:half] + down_first + up_first, own[half:] + up_last + down_last])


def on_device(observed, noise_precision, mid_basis, root_basis, mid_prior, root_prior, leaf_count):
    slots, knots = mid_basis.shape
    root_knots = root_basis.shape[1]
    regions, groups = lax.axis_size("region"), lax.axis_size("group")
    deep, wide, cores = 8, regions // 8, 2
    region, group = lax.axis_index("region"), lax.axis_index("group")
    x, z = lax.div(region, deep), region & (deep - 1)
    y, core = lax.div(group, cores), group & 1
    chunks = slots // BLOCK
    noise = noise_precision.reshape(chunks, BLOCK)
    values = observed.reshape(chunks, BLOCK)
    blocks = knots // BLOCK
    packed = len(lower_blocks(blocks)) * BLOCK
    share = packed // regions
    group_share = packed // groups
    params = pltpu.CompilerParams(vmem_limit_bytes=VMEM_LIMIT)
    pieces, gram_pieces = 4, 4
    smem = pl.BlockSpec(memory_space=pltpu.SMEM)
    far = pl.BlockSpec(memory_space=pltpu.HBM)
    square = pltpu.VMEM((knots, knots), f32)
    rows = pltpu.VMEM((slots, knots), f32)
    waits = pltpu.SemaphoreType.DMA((pieces,))

    def cost(flops, size):
        return pl.CostEstimate(flops=int(flops), bytes_accessed=int(size), transcendentals=0)

    gram_flops = 2 * slots * knots * knots
    slab = knots // regions * (root_knots // BLOCK)
    *parts, root_parts, mid_diagonal, root_diagonal = pl.pallas_call(
        functools.partial(gram_kernel, gram_pieces),
        out_shape=(
            jax.ShapeDtypeStruct((deep, TILE + share + slab, BLOCK), f32),
            *[jax.ShapeDtypeStruct((deep // 2, TILE + share + slab, BLOCK), f32)] * 6,
            jax.ShapeDtypeStruct((groups, group_share, BLOCK), f32),
            jax.ShapeDtypeStruct((1, knots), f32),
            jax.ShapeDtypeStruct((1, root_knots), f32),
        ),
        in_specs=[smem, smem] + whole(4) + [far, far],
        out_specs=tuple(whole(10)),
        scratch_shapes=[
            pltpu.VMEM((regions, TILE + share + slab, BLOCK), f32),
            rows,
            rows,
            pltpu.VMEM((knots, 2 * (knots + root_knots)), f32),
            square,
            pltpu.VMEM((root_knots, 2 * root_knots), f32),
            waits,
            waits,
        ],
        compiler_params=params,
        cost_estimate=cost(7 * gram_flops, 8 * slots * knots),
        name="gram",
    )(x.reshape(1), leaf_count, noise, values, mid_prior, root_prior.reshape(1, root_knots), mid_basis, root_basis)
    root_part = root_parts.reshape(groups // cores, cores, group_share, BLOCK)
    root_part = part(root_part, core, 1) + swapped(part(root_part, 1 - core, 1), "group", 1)
    root_part = summed_over_line(root_part, "group", y, cores, groups // cores)
    fine = group_share // wide
    root_part = summed_over_line(
        root_part.reshape(wide, fine, BLOCK), "region", x, deep, wide
    )
    own, *others = parts
    parts = summed_around(own, others[:2], others[2:4], others[4:], "region", deep, wide)
    lines = [[a * deep + b for b in range(deep)] for a in range(wide)]

    def along_z(value):
        return lax.all_to_all(value, "region", 0, 0, tiled=True, axis_index_groups=lines)

    shares = along_z(parts).sum(axis=0)
    sent = jnp.concatenate([shares[TILE:], root_part])
    every_z = along_z(jnp.broadcast_to(sent[None], (deep, share + slab + fine, BLOCK)))

    def along_x(value):
        return [value] + [moved_by(value, "region", d, deep, wide) for d in range(1, wide)]

    mid_blocks = along_x(every_z[:, :share])
    cross_rows = every_z[:, share : share + slab].reshape(deep * slab, BLOCK)
    root_rows = every_z[:, share + slab :].sum(axis=0)
    cross_blocks = along_x(jnp.concatenate([cross_rows, root_rows]))

    pairs = blocks * (blocks - 1) // 2
    inverse, factor = pl.pallas_call(
        mid_factor_kernel,
        out_shape=(
            jax.ShapeDtypeStruct((knots, BLOCK), f32),
            jax.ShapeDtypeStruct((pairs * BLOCK, BLOCK), f32),
        ),
        in_specs=[smem] + whole(1 + wide),
        out_specs=tuple(whole(2)),
        scratch_shapes=[pltpu.VMEM((regions, share, BLOCK), f32)],
        compiler_params=params,
        cost_estimate=cost(2e10, 3e6),
        name="mid_factor",
    )(x.reshape(1), mid_diagonal, *mid_blocks)
    reduced, solved, line, root_pieces = pl.pallas_call(
        functools.partial(schur_kernel, deep),
        out_shape=(
            jax.ShapeDtypeStruct((groups, group_share + TILE, BLOCK), f32),
            jax.ShapeDtypeStruct((knots, root_knots), f32),
            jax.ShapeDtypeStruct((blocks * TILE, BLOCK), f32),
            jax.ShapeDtypeStruct((wide, fine, BLOCK), f32),
        ),
        in_specs=[smem] + whole(3 + wide),
        out_specs=tuple(whole(4)),
        scratch_shapes=[square, square],
        compiler_params=params,
        cost_estimate=cost(4e9, 4e6),
        name="schur",
    )(x.reshape(1), inverse, factor, shares[:TILE], *cross_blocks)
    root_part = root_pieces.reshape(group_share, BLOCK)
    full, vector = pl.pallas_call(
        back_kernel,
        out_shape=(
            jax.ShapeDtypeStruct((knots, root_knots), f32),
            jax.ShapeDtypeStruct((TILE, knots), f32),
        ),
        in_specs=whole(3),
        out_specs=tuple(whole(2)),
        compiler_params=params,
        cost_estimate=cost(4e9, 3e6),
        name="mid_back_substitution",
    )(solved, factor, line)

    summed = exchange(reduced, "group").sum(axis=0)
    root_all = exchange(for_everyone(summed[:group_share] + root_part, "group"), "group")

    root_means, mid_means, fit = pl.pallas_call(
        functools.partial(root_kernel, pieces),
        out_shape=(
            jax.ShapeDtypeStruct((1, root_knots), f32),
            jax.ShapeDtypeStruct((1, knots), f32),
            jax.ShapeDtypeStruct((chunks, BLOCK), f32),
        ),
        in_specs=whole(5) + [far, far],
        out_specs=tuple(whole(3)),
        scratch_shapes=[rows, rows, waits, waits],
        compiler_params=params,
        cost_estimate=cost(2.5e10, 8 * slots * knots),
        name="root_solve_and_fit",
    )(root_all, summed[group_share:], root_diagonal, full, vector, mid_basis, root_basis)

    mid_slab = knots // regions
    middle = lax.dynamic_slice_in_dim(mid_means, region * mid_slab, mid_slab, 1)
    return root_means.reshape(root_knots), middle, fit.reshape(slots)


def solution(mesh):
    return jax.shard_map(
        on_device,
        mesh=mesh,
        in_specs=(
            P(("group", "region")),
            P(("group", "region")),
            P(("group", "region"), None),
            P(("group", "region"), None),
            P("group", None),
            P(),
            P("group", "region"),
        ),
        out_specs=(P(), P("group", "region"), P(("group", "region"))),
        check_vma=False,
    )
```
